256 devices in a mesh: px: 32 (over z_lo, y, core), py: 8 (over x, z_hi).
Axes of the slice: x: 4, y: 4, z: 8 (z_hi: 2, z_lo: 4; z = z_hi * 4 + z_lo), core: 2. Of those that a mesh axis runs over, the one named last changes fastest.
Arguments:
- nodal_field: float32 [32, 8, 4096], P('px', 'py'), may hold values from -6 to 6
- element_matrix: float32 [32, 8, 16, 16384], P('px', 'py'), may hold values from -0.75 to 0.75
- connectivity: int32 [32, 8, 4, 16384], P('px', 'py'), may hold values from 0 to 4079
- face_nodes: int32 [32, 8, 4, 256], P('px', 'py'), may hold values from 0 to 4095, as said below
- panel_node: int32 [32, 8, 512], P('px', 'py'), may hold values from 0 to 4095
- panel_weight: float32 [32, 8, 512], P('px', 'py'), may hold values from 0.02 to 0.08
- centroid: float32 [32, 8, 3, 512], P('px', 'py'), may hold values from -1 to 1
- panel_normal: float32 [32, 8, 3, 512], P('px', 'py'), may hold values from -1 to 1, as said below
- panel_count: int32 [32, 8], replicated, may hold values from 256 to 512, as said below
- target_index: int32 [32, 8, 256], P('px', 'py'), may hold values from 0 to 255
- round_owner: int32 [8], replicated, may hold values from 0 to 31, as said below
Outputs:
- fem_image: float32 [32, 8, 4096], P('px', 'py')
- bem_image: float32 [32, 8, 256], P('px', 'py')
The draws below stay inside these ranges and needn't reach their ends.
Inputs may be any that keep to these rules, and one draw needn't show every extreme that they name: `face_nodes`: the 1024 entries of one partition are distinct. `panel_count`: some owner has all 512 slots live. `round_owner`: distinct rows. `panel_normal`: unit vectors.
All inputs are finite; a program needn't handle non-finite values.
Results may differ from the reference program's by a relative error of at most 0.0001.
Values sent between devices are 32-bit elements; how exact they have to be, the bound alone decides.
A program may use at most 64 MiB of HBM per device.

```python
import math
import jax
import jax.numpy as jnp
from jax import lax

NL = 4096
ELEMS = 16384
FACE = 256
PAN = 512
TGT = 256
ROUNDS = 8
GX = 32
GY = 8


def draw_face_nodes(key, part):
    keys = jax.random.split(key, GX * GY)
    chosen = jax.vmap(lambda single: jax.random.permutation(single, NL)[:4 * FACE])(keys)
    return chosen.reshape(GX, GY, 4, FACE).astype(jnp.int32)


def draw_panel_count(key, part):
    counts = jax.random.randint(key, (GX * GY,), PAN // 2, PAN + 1)
    fullest = jax.random.randint(jax.random.fold_in(key, 7), (), 0, GX * GY)
    counts = counts.at[fullest].set(PAN)
    return counts.reshape(GX, GY).astype(jnp.int32)


def draw_panel_normal(key, part):
    height = jax.random.uniform(jax.random.fold_in(key, 1), (GX, GY, 1, PAN), jnp.float32, -1.0, 1.0)
    turn = jax.random.uniform(jax.random.fold_in(key, 2), (GX, GY, 1, PAN), jnp.float32, -math.pi, math.pi)
    radial = jnp.sqrt(jnp.maximum(1.0 - height * height, 0.0))
    return jnp.concatenate([radial * jnp.cos(turn), radial * jnp.sin(turn), height], axis=2).astype(jnp.float32)


def draw_round_owner(key, part):
    key = jax.random.fold_in(key, 5)
    middle = jax.random.permutation(key, GX - 2)[:ROUNDS - 2].astype(jnp.int32) + 1
    ends = jnp.array([0, GX - 1], jnp.int32)
    chosen = jnp.concatenate([ends, middle])
    order = jax.random.permutation(jax.random.fold_in(key, 11), ROUNDS)
    return chosen[order].astype(jnp.int32)


def touch_ends(result, stream_key, least, top_value):
    longest = result.shape.index(max(result.shape))
    spots = []
    for shift in (0, 1):
        where = [jax.random.randint(jax.random.fold_in(stream_key, axis), (), 0, length) for axis, length in enumerate(result.shape)]
        where[longest] = (where[longest] + shift) % result.shape[longest]
        spots.append(tuple(where))
    return result.at[spots[0]].set(least).at[spots[1]].set(top_value)


def shard_levels(own_key, shape, shards, smallest, top_value):
    def one(axis_at, shards_of):
        heights = jax.random.uniform(jax.random.fold_in(jax.random.fold_in(own_key, 6), axis_at), (shards_of,), jnp.float32, smallest / len(shards), top_value / len(shards))
        return jnp.repeat(jnp.exp(heights), shape[axis_at] // shards_of).reshape((-1,) + (1,) * (len(shape) - axis_at - 1))

    factor_of = one(*shards[0])
    for cut in shards[1:]:
        factor_of = factor_of * one(*cut)
    return factor_of


def centred(rng, shape, scale, most, shards=(), kind=jnp.bfloat16):
    entries = scale * jax.random.normal(rng, shape, jnp.float32)
    if shards:
        entries = entries * shard_levels(rng, shape, shards, -0.22, 0.18)
    return jnp.clip(entries, -most, most).astype(kind)


def setup_inputs(seed: int = 0) -> dict:
    splits = jax.random.split(jax.random.key(seed), 12)
    return {
        "nodal_field": centred(splits[0], (GX, GY, NL), 1.0, 6.0, ((0, 32), (1, 8)), jnp.float32),
        "element_matrix": centred(splits[1], (GX, GY, 16, ELEMS), 0.125, 0.75, ((0, 32), (1, 8)), jnp.float32),
        "connectivity": touch_ends(jax.random.randint(splits[2], (GX, GY, 4, ELEMS), 0, NL - 16), jax.random.fold_in(splits[2], 1), 0, (NL - 16) - 1).astype(jnp.int32),
        "face_nodes": draw_face_nodes(jax.random.fold_in(splits[11], 71), 0),
        "panel_node": touch_ends(jax.random.randint(splits[4], (GX, GY, PAN), 0, NL), jax.random.fold_in(splits[4], 1), 0, NL - 1).astype(jnp.int32),
        "panel_weight": jnp.clip(jnp.exp(math.log(0.08) - 1.3862944 * jax.random.uniform(splits[5], (GX, GY, PAN), jnp.float32) ** shard_levels(splits[5], (GX, GY, PAN), ((0, 32), (1, 8)), -0.2, 0.2)), 0.02, 0.08),
        "centroid": jnp.clip(jax.random.uniform(splits[6], (GX, GY, 3, PAN), jnp.float32, -1.0, 1.0) * shard_levels(splits[6], (GX, GY, 3, PAN), ((0, 32), (1, 8)), -0.4, 0.0), -1.0, 1.0),
        "panel_normal": draw_panel_normal(jax.random.fold_in(splits[11], 71), 0),
        "panel_count": draw_panel_count(jax.random.fold_in(splits[11], 71), 0),
        "target_index": touch_ends(jax.random.randint(splits[9], (GX, GY, TGT), 0, PAN // 2), jax.random.fold_in(splits[9], 1), 0, (PAN // 2) - 1).astype(jnp.int32),
        "round_owner": draw_round_owner(jax.random.fold_in(splits[11], 71), 0),
    }


SMOOTH_SQ = 0.01
FOUR_PI = 4.0 * math.pi

def partition_apply(nodal, matrices, connect):
    values = nodal[connect]
    blocks = matrices.reshape(4, 4, -1)
    element_out = lax.optimization_barrier(jnp.sum(blocks * values[None, :, :], axis=1))
    return jnp.zeros_like(nodal).at[connect.reshape(-1)].add(element_out.reshape(-1))

def kernel_sum(target_pos, source_pos, source_normal, source_weighted):
    offset = target_pos[:, :, None] - source_pos[:, None, :]
    dist_sq = lax.optimization_barrier(jnp.sum(offset * offset, axis=0))
    smoothed = dist_sq + SMOOTH_SQ
    normal_dot = lax.optimization_barrier(jnp.sum(source_normal[:, None, :] * offset, axis=0))
    contrib = normal_dot * source_weighted[None, :] / (FOUR_PI * smoothed * jnp.sqrt(smoothed))
    return lax.optimization_barrier(jnp.sum(contrib, axis=1))

def reference(nodal_field, element_matrix, connectivity, face_nodes, panel_node, panel_weight, centroid, panel_normal, panel_count, target_index, round_owner):
    partial_image = lax.map(lambda grid_row: jax.vmap(partition_apply)(*grid_row), (nodal_field, element_matrix, connectivity))
    outgoing = jax.vmap(jax.vmap(lambda image, ids: image[ids]))(partial_image, face_nodes)
    zero_row = jnp.zeros((1, GY, FACE), outgoing.dtype)
    zero_col = jnp.zeros((GX, 1, FACE), outgoing.dtype)
    from_low_x = jnp.concatenate([zero_row, outgoing[:-1, :, 1]], axis=0)
    from_high_x = jnp.concatenate([outgoing[1:, :, 0], zero_row], axis=0)
    from_low_y = jnp.concatenate([zero_col, outgoing[:, :-1, 3]], axis=1)
    from_high_y = jnp.concatenate([outgoing[:, 1:, 2], zero_col], axis=1)
    received = jnp.stack([from_low_x, from_high_x, from_low_y, from_high_y], axis=2)
    fem_image = jax.vmap(jax.vmap(lambda image, ids, extra: image.at[ids.reshape(-1)].add(extra.reshape(-1))))(partial_image, face_nodes, received)
    trace = jax.vmap(jax.vmap(lambda nodal, ids: nodal[ids]))(nodal_field, panel_node)
    slot_ids = jnp.arange(PAN, dtype=jnp.int32)
    is_live = slot_ids[None, None, :] < panel_count[:, :, None]
    weighted = jnp.where(is_live, panel_weight * trace, jnp.float32(0.0))
    target_pos = jax.vmap(jax.vmap(lambda place, ids: place[:, ids]))(centroid, target_index)
    target_trace = jax.vmap(jax.vmap(lambda values, ids: values[ids]))(trace, target_index)
    potential = jnp.zeros((GX, GY, TGT), jnp.float32)
    for round_no in range(ROUNDS):
        owner_row = round_owner[round_no]
        source_pos = centroid[owner_row]
        source_normal = panel_normal[owner_row]
        source_weighted = weighted[owner_row]
        potential = potential + lax.map(lambda grid_row: jax.vmap(kernel_sum)(grid_row, source_pos, source_normal, source_weighted), target_pos)
    bem_image = potential - 0.5 * target_trace
    return (fem_image, bem_image)
```

```python
import functools
import math

import jax
import jax.numpy as jnp
from jax import lax
from jax.experimental import pallas as pl
from jax.experimental.pallas import tpu as pltpu
from jax.sharding import PartitionSpec as P

F32 = jnp.float32
BF16 = jnp.bfloat16
MESH = pl.DeviceIdType.MESH

GX, GY = 32, 8
ROUNDS = 8
CHIPS = GX // 2
ROWS = 512
HI, LO = 32, 128
PAIRS = 8
STEPS = ROWS // (8 * PAIRS)
SMOOTH_SQ = 0.01
FOUR_PI = 4.0 * math.pi


def lookup(rows, index):
    lo, hi = index & (LO - 1), index >> 7
    total = jnp.zeros(index.shape, F32)
    for r, row in enumerate(rows):
        picked = jnp.take_along_axis(jnp.broadcast_to(row, index.shape), lo, axis=1)
        total = jnp.where(hi == r, picked, total)
    return total


def table(ref):
    return [ref[r : r + 1, :] for r in range(HI)]


def stack(x, count):
    return jnp.concatenate([x] * count, axis=0)


def one_hots(index_rows, value_rows):
    io_hi = lax.broadcasted_iota(jnp.int32, (HI, 128), 0).astype(F32).astype(BF16)
    io_lo = lax.broadcasted_iota(jnp.int32, (LO, 128), 0).astype(F32).astype(BF16)
    zero_hi, zero_lo = jnp.zeros((HI, 128), BF16), jnp.zeros((LO, 128), BF16)
    one_lo = jnp.ones((LO, 128), BF16)
    left, right = [], []
    for index, value in zip(index_rows, value_rows):
        hi = jnp.broadcast_to((index >> 7).astype(F32), (16, 128)).astype(BF16)
        lo = jnp.broadcast_to((index & (LO - 1)).astype(F32), (16, 128)).astype(BF16)
        value = jnp.broadcast_to(value, (16, 128))
        upper = value.astype(BF16)
        lower = (value - upper.astype(F32)).astype(BF16)
        at_hi = stack(hi, HI // 16) == io_hi
        left.append(
            jnp.concatenate(
                [
                    jnp.where(at_hi, stack(upper, HI // 16), zero_hi),
                    jnp.where(at_hi, stack(lower, HI // 16), zero_hi),
                ],
                axis=0,
            )
        )
        right.append(jnp.where(stack(lo, LO // 16) == io_lo, one_lo, zero_lo))
    return jnp.concatenate(left, axis=1), jnp.concatenate(right, axis=1)


def scatter_product(index_rows, value_rows):
    left, right = one_hots(index_rows, value_rows)
    return lax.dot_general(left, right, (((1,), (1,)), ((), ())), preferred_element_type=F32)


def kernel(
    count_ref, owner_ref, nodal_ref, conn_ref, matrix_ref, face_ref, node_ref, weight_ref,
    centroid_ref, normal_ref, target_ref,
    fem_ref, bem_ref,
    block, gathered, value, total, partial, sent, incoming, place, small, potential,
    send_sem, recv_sem, face_send, face_recv,
):
    px, py = lax.axis_index("px"), lax.axis_index("py")
    core = lax.rem(px, 2)
    sibling = px + 1 - 2 * core
    low_x, high_x = lax.rem(px + GX - 1, GX), lax.rem(px + 1, GX)
    low_y, high_y = lax.rem(py + GY - 1, GY), lax.rem(py + 1, GY)
    across = jnp.where(core == 0, low_x, high_x)

    barrier = pltpu.get_barrier_semaphore()

    @pl.loop(1, CHIPS)
    def _(d):
        pl.semaphore_signal(
            barrier, inc=1, device_id=(lax.rem(px + 2 * d, GX), py), device_id_type=MESH
        )

    for device in ((sibling, py), (across, py), (px, low_y), (px, high_y)):
        pl.semaphore_signal(barrier, inc=1, device_id=device, device_id_type=MESH)

    sublane = lax.broadcasted_iota(jnp.int32, (8, 128), 0)
    lane = lax.broadcasted_iota(jnp.int32, (8, 128), 1)

    small[0:4, :] = node_ref[...]
    small[4:8, :] = node_ref[...]
    trace = lookup(table(nodal_ref), small[...])
    live = count_ref[py, px]
    slot = (sublane & 3) * 128 + lane
    weight = jnp.concatenate([weight_ref[...], weight_ref[...]], axis=0)
    weighted = jnp.where(slot < live, weight * trace, 0.0)
    block[0:12, :] = centroid_ref[...]
    block[12:24, :] = normal_ref[...] * stack(weighted[0:4, :], 3)

    pl.semaphore_wait(barrier, CHIPS + 3)

    def to_chip(d, source):
        return pltpu.make_async_remote_copy(
            src_ref=block,
            dst_ref=gathered.at[source],
            send_sem=send_sem.at[d],
            recv_sem=recv_sem.at[source],
            device_id=(lax.rem(px + 2 * d, GX), py),
            device_id_type=MESH,
        )

    def to_sibling(d, source, held):
        return pltpu.make_async_remote_copy(
            src_ref=held,
            dst_ref=gathered.at[source],
            send_sem=send_sem.at[CHIPS + d],
            recv_sem=recv_sem.at[source],
            device_id=(sibling, py),
            device_id_type=MESH,
        )

    @pl.loop(1, CHIPS)
    def _(d):
        to_chip(d, px).start()

    to_sibling(0, px, block).start()
    gathered[px] = block[...]

    for i in range(4):
        small[2 * i : 2 * i + 2, :] = target_ref[...]
    targets = small[...]
    target_trace = lookup([trace[k : k + 1, :] for k in range(2)], targets)
    for c in range(3):
        where = lookup([block[4 * c + k : 4 * c + k + 1, :] for k in range(2)], targets)
        for half in range(2):
            place[c, 128 * half : 128 * half + 128, :] = jnp.broadcast_to(
                where[half : half + 1, :], (128, 128)
            ).T

    total[...] = jnp.zeros_like(total)
    odd, second, fourth = (sublane & 1) == 1, (sublane & 2) == 2, (sublane & 4) == 4

    @pl.loop(0, STEPS)
    def _(step):
        base = step * PAIRS
        index_rows, value_rows = [], []
        for u in range(PAIRS):
            at = pl.multiple_of((base + u) * 8, 8)
            nodes = conn_ref[pl.ds(at, 8), :]
            values = lookup(table(nodal_ref), nodes)
            swapped = pltpu.roll(values, 4, 0)
            folded = []
            for chunk in range(2):
                both = jnp.where(fourth, swapped, values) if chunk == 0 else jnp.where(fourth, values, swapped)
                lanes = pl.ds(pl.multiple_of((base + u) * 256 + 128 * chunk, 128), 128)
                first = matrix_ref[0:8, lanes] * both
                last = matrix_ref[8:16, lanes] * both
                folded.append(
                    jnp.where(second, last + pltpu.roll(last, 2, 0), first + pltpu.roll(first, 6, 0))
                )
            value[8 * u : 8 * u + 8, :] = jnp.where(
                odd, folded[1] + pltpu.roll(folded[1], 1, 0), folded[0] + pltpu.roll(folded[0], 7, 0)
            )
            for chunk in range(2):
                for corner in range(4):
                    index_rows.append(conn_ref[pl.ds(at + 4 * chunk + corner, 1), :])
                    row = 8 * u + (0, 4, 2, 6)[corner] + chunk
                    value_rows.append(value[row : row + 1, :])
        total[...] += scatter_product(index_rows, value_rows)

    partial[...] = total[0:HI, :] + total[HI : 2 * HI, :]

    outgoing = lookup(table(partial), face_ref[...])
    for f in range(4):
        for half in range(2):
            sent[f, half : half + 1, :] = outgoing[4 * half + f : 4 * half + f + 1, :]
    neighbours = ((low_x, py), (high_x, py), (px, low_y), (px, high_y))
    faces = [
        pltpu.make_async_remote_copy(
            src_ref=sent.at[f],
            dst_ref=incoming.at[f ^ 1],
            send_sem=face_send.at[f],
            recv_sem=face_recv.at[f ^ 1],
            device_id=neighbours[f],
            device_id_type=MESH,
        )
        for f in range(4)
    ]
    for face in faces:
        face.start()

    @pl.loop(1, CHIPS)
    def _(d):
        source = lax.rem(px + GX - 2 * d, GX)
        to_chip(d, source).wait_recv()
        to_sibling(d, source, gathered.at[source]).start()

    @pl.loop(0, CHIPS)
    def _(d):
        source = lax.rem(sibling + GX - 2 * d, GX)
        to_sibling(d, source, gathered.at[source]).wait_recv()

    @pl.loop(0, 8)
    def _(part):
        spots = [
            [place[c, pl.ds(pl.multiple_of(32 * part + 8 * g, 8), 8), :] for c in range(3)]
            for g in range(4)
        ]

        def one_round(r, sums):
            owner = owner_ref[r]
            sums = list(sums)
            for k in range(4):
                rows = [
                    jnp.broadcast_to(gathered[owner, 4 * c + k : 4 * c + k + 1, :], (8, 128))
                    for c in range(6)
                ]
                for g in range(4):
                    dx, dy, dz = (spots[g][c] - rows[c] for c in range(3))
                    inverse = lax.rsqrt(dx * dx + dy * dy + dz * dz + SMOOTH_SQ)
                    along = rows[3] * dx + rows[4] * dy + rows[5] * dz
                    sums[g] = sums[g] + along * (inverse * inverse * inverse)
            return tuple(sums)

        sums = lax.fori_loop(0, ROUNDS, one_round, (jnp.zeros((8, 128), F32),) * 4)
        for g in range(4):
            potential[pl.ds(pl.multiple_of(32 * part + 8 * g, 8), 8), :] = sums[g]

    for half in range(2):
        summed = jnp.sum(potential[128 * half : 128 * half + 128, :].T, axis=0, keepdims=True)
        bem_ref[half : half + 1, :] = (
            summed * (1.0 / FOUR_PI) - 0.5 * target_trace[half : half + 1, :]
        )

    for face in faces:
        face.wait_recv()
    present = (px > 0, px < GX - 1, py > 0, py < GY - 1)
    index_rows, value_rows = [], []
    for f in range(4):
        for half in range(2):
            row = 4 * half + f
            index_rows.append(face_ref[row : row + 1, :])
            value_rows.append(jnp.where(present[f], incoming[f, half : half + 1, :], 0.0))
    added = scatter_product(index_rows, value_rows)
    fem_ref[...] = partial[...] + added[0:HI, :] + added[HI : 2 * HI, :]

    for face in faces:
        face.wait_send()

    @pl.loop(1, CHIPS)
    def _(d):
        to_chip(d, px).wait_send()

    @pl.loop(0, CHIPS)
    def _(d):
        to_sibling(d, px, block).wait_send()


def per_device(
    nodal_field, element_matrix, connectivity, face_nodes, panel_node, panel_weight,
    centroid, panel_normal, panel_count, target_index, round_owner,
):
    vmem = pl.BlockSpec(memory_space=pltpu.VMEM)
    smem = pl.BlockSpec(memory_space=pltpu.SMEM)
    connect = connectivity[0, 0].reshape(4, 128, 128).transpose(1, 0, 2).reshape(ROWS, 128)
    fem, bem = pl.pallas_call(
        kernel,
        out_shape=(
            jax.ShapeDtypeStruct((HI, LO), F32),
            jax.ShapeDtypeStruct((2, 128), F32),
        ),
        in_specs=[smem, smem] + [vmem] * 9,
        out_specs=(vmem, vmem),
        scratch_shapes=[
            pltpu.VMEM((24, 128), F32),
            pltpu.VMEM((GX, 24, 128), F32),
            pltpu.VMEM((8 * PAIRS, 128), F32),
            pltpu.VMEM((2 * HI, LO), F32),
            pltpu.VMEM((HI, LO), F32),
            pltpu.VMEM((4, 2, 128), F32),
            pltpu.VMEM((4, 2, 128), F32),
            pltpu.VMEM((3, 256, 128), F32),
            pltpu.VMEM((8, 128), jnp.int32),
            pltpu.VMEM((256, 128), F32),
            pltpu.SemaphoreType.DMA((2 * CHIPS,)),
            pltpu.SemaphoreType.DMA((GX,)),
            pltpu.SemaphoreType.DMA((4,)),
            pltpu.SemaphoreType.DMA((4,)),
        ],
        compiler_params=pltpu.CompilerParams(
            collective_id=0, has_side_effects=True, vmem_limit_bytes=32 * 1024 * 1024
        ),
        name="apply",
    )(
        panel_count.T,
        round_owner,
        nodal_field.reshape(HI, LO),
        connect,
        element_matrix[0, 0],
        face_nodes[0, 0].reshape(4, 2, 128).transpose(1, 0, 2).reshape(8, 128),
        panel_node.reshape(4, 128),
        panel_weight.reshape(4, 128),
        centroid.reshape(12, 128),
        panel_normal.reshape(12, 128),
        target_index.reshape(2, 128),
    )
    return fem.reshape(1, 1, HI * LO), bem.reshape(1, 1, 256)


def solution(mesh):
    split = P("px", "py")
    return jax.shard_map(
        per_device,
        mesh=mesh,
        in_specs=(split,) * 8 + (P(), split, P()),
        out_specs=(split, split),
        check_vma=False,
    )
```

```python
import functools
import math

import jax
import jax.numpy as jnp
from jax import lax
from jax.experimental import pallas as pl
from jax.experimental.pallas import tpu as pltpu
from jax.sharding import PartitionSpec as P

F32 = jnp.float32
BF16 = jnp.bfloat16
MESH = pl.DeviceIdType.MESH

GX, GY = 32, 8
ROUNDS = 8
BINS = 64
ROWS = 512
HI, LO = 32, 128
PAIRS = 32
STEPS = ROWS // (8 * PAIRS)
GROUPS = 8
SMOOTH_SQ = 0.01
FOUR_PI = 4.0 * math.pi


def lookup(rows, index):
    lo, hi = index & (LO - 1), index >> 7
    total = jnp.zeros(index.shape, F32)
    for r, row in enumerate(rows):
        picked = jnp.take_along_axis(jnp.broadcast_to(row, index.shape), lo, axis=1)
        total = jnp.where(hi == r, picked, total)
    return total


def table(ref):
    return [ref[r : r + 1, :] for r in range(HI)]


def stack(x, count):
    return jnp.concatenate([x] * count, axis=0)


def one_hots(index_rows, value_rows):
    bins = lax.broadcasted_iota(jnp.int32, (BINS, 128), 0).astype(F32).astype(BF16)
    zero, one = jnp.zeros((BINS, 128), BF16), jnp.ones((BINS, 128), BF16)
    left, right = [], []
    for index, value in zip(index_rows, value_rows):
        hi = (index >> 7) | ((index & 64) >> 1)
        hi = jnp.broadcast_to(hi.astype(F32), (16, 128)).astype(BF16)
        lo = jnp.broadcast_to((index & 63).astype(F32), (16, 128)).astype(BF16)
        value = jnp.broadcast_to(value, (16, 128))
        upper = value.astype(BF16)
        lower = (value - upper.astype(F32)).astype(BF16)
        at_hi = stack(hi, BINS // 16) == bins
        left.append(
            jnp.concatenate(
                [
                    jnp.where(at_hi, stack(upper, BINS // 16), zero),
                    jnp.where(at_hi, stack(lower, BINS // 16), zero),
                ],
                axis=0,
            )
        )
        right.append(jnp.where(stack(lo, BINS // 16) == bins, one, zero))
    return jnp.concatenate(left, axis=1), jnp.concatenate(right, axis=1)


def scatter_product(index_rows, value_rows):
    left, right = one_hots(index_rows, value_rows)
    return lax.dot_general(left, right, (((1,), (1,)), ((), ())), preferred_element_type=F32)


def as_table(sums):
    bins = sums[0:BINS, :] + sums[BINS : 2 * BINS, :]
    return jnp.concatenate([bins[0:HI, :], bins[HI:BINS, :]], axis=1)


def kernel(
    count_hbm, owner_hbm, nodal_hbm, conn_hbm, matrix_hbm, face_hbm, node_hbm, weight_hbm,
    centroid_hbm, normal_hbm, target_hbm,
    fem_ref, bem_ref,
    count_ref, owner_ref, nodal_ref, conn_ref, matrix_ref, face_ref, node_ref, weight_ref,
    centroid_ref, normal_ref, target_ref,
    halves, gathered, value, total, partial, sent, incoming, spots_out, spots_in, place,
    potential, sums_out, sums_in,
    load_sem, conn_sem, matrix_sem, send_sem, recv_sem, face_send, face_recv, pair_send, pair_recv,
):
    px, py = lax.axis_index("px"), lax.axis_index("py")
    core = px & 1
    sibling = px + 1 - 2 * core
    low_y, high_y = (py + GY - 1) & (GY - 1), (py + 1) & (GY - 1)

    names = ("nodal", "node", "count", "weight", "centroid", "normal", "target", "face", "owner")
    sources = (nodal_hbm, node_hbm, count_hbm, weight_hbm, centroid_hbm, normal_hbm, target_hbm, face_hbm, owner_hbm)
    places = (nodal_ref, node_ref, count_ref, weight_ref, centroid_ref, normal_ref, target_ref, face_ref, owner_ref)
    loads = {
        name: pltpu.make_async_copy(source, where, load_sem.at[i])
        for i, (name, source, where) in enumerate(zip(names, sources, places))
    }

    def conn_load(step):
        rows = pl.ds(pl.multiple_of(step * 8 * PAIRS, 8), 8 * PAIRS)
        return pltpu.make_async_copy(conn_hbm.at[rows], conn_ref.at[rows], conn_sem.at[step])

    def matrix_load(step):
        lanes = pl.ds(pl.multiple_of(step * 256 * PAIRS, 128), 256 * PAIRS)
        return pltpu.make_async_copy(
            matrix_hbm.at[:, lanes], matrix_ref.at[:, lanes], matrix_sem.at[step]
        )

    for name in names:
        loads[name].start()

    @pl.loop(0, STEPS)
    def _(step):
        conn_load(step).start()
        matrix_load(step).start()

    barrier = pltpu.get_barrier_semaphore()

    @pl.loop(1, GX)
    def _(d):
        pl.semaphore_signal(
            barrier, inc=1, device_id=((px + d) & (GX - 1), py), device_id_type=MESH
        )

    for column in (low_y, high_y):
        pl.semaphore_signal(barrier, inc=1, device_id=(px, column), device_id_type=MESH)

    sublane = lax.broadcasted_iota(jnp.int32, (8, 128), 0)
    lane = lax.broadcasted_iota(jnp.int32, (8, 128), 1)

    for name in ("nodal", "node", "count", "weight", "centroid", "normal", "target"):
        loads[name].wait()
    trace = lookup(table(nodal_ref), stack(node_ref[...], 2))
    live = count_ref[py, px]
    slot = (sublane & 3) * 128 + lane
    weighted = jnp.where(slot < live, stack(weight_ref[...], 2) * trace, 0.0)
    for h in range(2):
        for c in range(3):
            halves[h, 2 * c : 2 * c + 2, :] = centroid_ref[c, 2 * h : 2 * h + 2, :]
            halves[h, 6 + 2 * c : 8 + 2 * c, :] = (
                normal_ref[c, 2 * h : 2 * h + 2, :] * weighted[2 * h : 2 * h + 2, :]
            )

    targets = stack(target_ref[...], 4)
    target_trace = lookup([trace[k : k + 1, :] for k in range(2)], targets)
    for c in range(3):
        where = lookup([centroid_ref[c, k : k + 1, :] for k in range(2)], targets)
        spots_out[2 * c : 2 * c + 2, :] = where[0:2, :]

    pl.semaphore_wait(barrier, GX + 1)

    def to_other(d, source):
        target = (px + d) & (GX - 1)
        return pltpu.make_async_remote_copy(
            src_ref=halves.at[target & 1],
            dst_ref=gathered.at[source],
            send_sem=send_sem.at[d],
            recv_sem=recv_sem.at[source],
            device_id=(target, py),
            device_id_type=MESH,
        )

    def to_sibling(source, where, n):
        return pltpu.make_async_remote_copy(
            src_ref=source,
            dst_ref=where,
            send_sem=pair_send.at[n],
            recv_sem=pair_recv.at[n],
            device_id=(sibling, py),
            device_id_type=MESH,
        )

    send_spots = to_sibling(spots_out, spots_in, 0)
    send_sums = to_sibling(sums_out, sums_in, 1)

    @pl.loop(1, GX)
    def _(d):
        to_other(d, px).start()

    send_spots.start()
    gathered[px] = halves[core]

    def spread(ref, first):
        for c in range(3):
            for half in range(2):
                row = ref[2 * c + half : 2 * c + half + 1, :]
                rows = slice(first + 128 * half, first + 128 * half + 128)
                place[c, rows, :] = jnp.broadcast_to(row, (128, 128)).T

    total[...] = jnp.zeros_like(total)
    odd, second, fourth = (sublane & 1) == 1, (sublane & 2) == 2, (sublane & 4) == 4

    @pl.loop(0, STEPS)
    def _(step):
        conn_load(step).wait()
        matrix_load(step).wait()
        base = step * PAIRS
        index_rows, value_rows = [], []
        for u in range(PAIRS):
            at = pl.multiple_of((base + u) * 8, 8)
            nodes = conn_ref[pl.ds(at, 8), :]
            values = lookup(table(nodal_ref), nodes)
            swapped = pltpu.roll(values, 4, 0)
            folded = []
            for chunk in range(2):
                pair = (swapped, values) if chunk == 0 else (values, swapped)
                both = jnp.where(fourth, *pair)
                lanes = pl.ds(pl.multiple_of((base + u) * 256 + 128 * chunk, 128), 128)
                first = matrix_ref[0:8, lanes] * both
                last = matrix_ref[8:16, lanes] * both
                folded.append(
                    jnp.where(second, last + pltpu.roll(last, 2, 0), first + pltpu.roll(first, 6, 0))
                )
            value[8 * u : 8 * u + 8, :] = jnp.where(
                odd, folded[1] + pltpu.roll(folded[1], 1, 0), folded[0] + pltpu.roll(folded[0], 7, 0)
            )
            for chunk in range(2):
                for corner in range(4):
                    index_rows.append(conn_ref[pl.ds(at + 4 * chunk + corner, 1), :])
                    row = 8 * u + (0, 4, 2, 6)[corner] + chunk
                    value_rows.append(value[row : row + 1, :])
        total[...] += scatter_product(index_rows, value_rows)

    partial[...] = as_table(total[...])

    loads["face"].wait()
    outgoing = lookup(table(partial), face_ref[...])
    for f in range(4):
        for half in range(2):
            sent[f, half : half + 1, :] = outgoing[4 * half + f : 4 * half + f + 1, :]
    neighbours = (
        ((px + GX - 1) & (GX - 1), py),
        ((px + 1) & (GX - 1), py),
        (px, low_y),
        (px, high_y),
    )
    faces = [
        pltpu.make_async_remote_copy(
            src_ref=sent.at[f],
            dst_ref=incoming.at[f ^ 1],
            send_sem=face_send.at[f],
            recv_sem=face_recv.at[f ^ 1],
            device_id=neighbours[f],
            device_id_type=MESH,
        )
        for f in range(4)
    ]
    for face in faces:
        face.start()

    loads["owner"].wait()
    spread(spots_out, 256)
    send_spots.wait_recv()
    spread(spots_in, 0)

    @pl.loop(1, GX)
    def _(d):
        to_other(d, (px + GX - d) & (GX - 1)).wait_recv()

    def double_layer(first):
        @pl.loop(0, 32 // GROUPS)
        def _(part):
            at = [pl.multiple_of(8 * (GROUPS * part + g), 8) for g in range(GROUPS)]
            spots = [[place[c, pl.ds(first + at[g], 8), :] for c in range(3)] for g in range(GROUPS)]

            def one_round(r, sums):
                owner = owner_ref[r]
                sums = list(sums)
                for k in range(2):
                    rows = [
                        jnp.broadcast_to(gathered[owner, 2 * c + k : 2 * c + k + 1, :], (8, 128))
                        for c in range(6)
                    ]
                    for g in range(GROUPS):
                        dx, dy, dz = (spots[g][c] - rows[c] for c in range(3))
                        inverse = lax.rsqrt(dx * dx + dy * dy + dz * dz + SMOOTH_SQ)
                        along = rows[3] * dx + rows[4] * dy + rows[5] * dz
                        sums[g] = sums[g] + along * (inverse * inverse * inverse)
                return tuple(sums)

            sums = lax.fori_loop(
                0, ROUNDS, one_round, (jnp.zeros((8, 128), F32),) * GROUPS, unroll=2
            )
            for g in range(GROUPS):
                potential[pl.ds(at[g], 8), :] = sums[g]

        return [
            jnp.sum(potential[128 * half : 128 * half + 128, :].T, axis=0, keepdims=True)
            for half in range(2)
        ]

    for half, row in enumerate(double_layer(0)):
        sums_out[half : half + 1, :] = row
    send_sums.start()
    own = double_layer(256)
    send_sums.wait_recv()
    for half in range(2):
        bem_ref[half : half + 1, :] = (
            own[half] + sums_in[half : half + 1, :]
        ) * (1.0 / FOUR_PI) - 0.5 * target_trace[half : half + 1, :]

    send_spots.wait_send()
    send_sums.wait_send()

    @pl.loop(1, GX)
    def _(d):
        to_other(d, px).wait_send()

    for face in faces:
        face.wait_send()
    for face in faces:
        face.wait_recv()
    present = (px > 0, px < GX - 1, py > 0, py < GY - 1)
    index_rows, value_rows = [], []
    for f in range(4):
        for half in range(2):
            row = 4 * half + f
            index_rows.append(face_ref[row : row + 1, :])
            value_rows.append(jnp.where(present[f], incoming[f, half : half + 1, :], 0.0))
    fem_ref[...] = partial[...] + as_table(scatter_product(index_rows, value_rows))


def per_device(
    nodal_field, element_matrix, connectivity, face_nodes, panel_node, panel_weight,
    centroid, panel_normal, panel_count, target_index, round_owner,
):
    vmem = pl.BlockSpec(memory_space=pltpu.VMEM)
    hbm = pl.BlockSpec(memory_space=pl.ANY)
    i32 = jnp.int32
    connect = connectivity[0, 0].reshape(4, 128, 128).transpose(1, 0, 2).reshape(ROWS, 128)
    faces = face_nodes[0, 0].reshape(4, 2, 128).transpose(1, 0, 2).reshape(8, 128)
    fem, bem = pl.pallas_call(
        kernel,
        out_shape=(
            pltpu.VMEM((HI, LO), F32),
            pltpu.VMEM((2, 128), F32),
        ),
        in_specs=[hbm] * 11,
        out_specs=(vmem, vmem),
        scratch_shapes=[
            pltpu.SMEM((GY, GX), i32),
            pltpu.SMEM((ROUNDS,), i32),
            pltpu.VMEM((HI, LO), F32),
            pltpu.VMEM((ROWS, 128), i32),
            pltpu.VMEM((16, ROWS * 32), F32),
            pltpu.VMEM((8, 128), i32),
            pltpu.VMEM((4, 128), i32),
            pltpu.VMEM((4, 128), F32),
            pltpu.VMEM((3, 4, 128), F32),
            pltpu.VMEM((3, 4, 128), F32),
            pltpu.VMEM((2, 128), i32),
            pltpu.VMEM((2, 12, 128), F32),
            pltpu.VMEM((GX, 12, 128), F32),
            pltpu.VMEM((8 * PAIRS, 128), F32),
            pltpu.VMEM((2 * BINS, BINS), F32),
            pltpu.VMEM((HI, LO), F32),
            pltpu.VMEM((4, 2, 128), F32),
            pltpu.VMEM((4, 2, 128), F32),
            pltpu.VMEM((6, 128), F32),
            pltpu.VMEM((6, 128), F32),
            pltpu.VMEM((3, 512, 128), F32),
            pltpu.VMEM((256, 128), F32),
            pltpu.VMEM((2, 128), F32),
            pltpu.VMEM((2, 128), F32),
            pltpu.SemaphoreType.DMA((9,)),
            pltpu.SemaphoreType.DMA((STEPS,)),
            pltpu.SemaphoreType.DMA((STEPS,)),
            pltpu.SemaphoreType.DMA((GX,)),
            pltpu.SemaphoreType.DMA((GX,)),
            pltpu.SemaphoreType.DMA((4,)),
            pltpu.SemaphoreType.DMA((4,)),
            pltpu.SemaphoreType.DMA((2,)),
            pltpu.SemaphoreType.DMA((2,)),
        ],
        compiler_params=pltpu.CompilerParams(
            collective_id=0, has_side_effects=True, vmem_limit_bytes=60 * 1024 * 1024
        ),
        name="apply",
    )(
        panel_count.T,
        round_owner,
        nodal_field.reshape(HI, LO),
        connect,
        element_matrix.reshape(16, -1),
        faces,
        panel_node.reshape(4, 128),
        panel_weight.reshape(4, 128),
        centroid.transpose(0, 2, 1, 3).reshape(3, 4, 128),
        panel_normal.transpose(0, 2, 1, 3).reshape(3, 4, 128),
        target_index.reshape(2, 128),
    )
    return fem.reshape(1, 1, HI * LO), bem.reshape(1, 1, 256)


def solution(mesh):
    split = P("px", "py")
    return jax.shard_map(
        per_device,
        mesh=mesh,
        in_specs=(split,) * 8 + (P(), split, P()),
        out_specs=(split, split),
        check_vma=False,
    )
```

```python
import functools
import math

import jax
import jax.numpy as jnp
from jax import lax
from jax.experimental import pallas as pl
from jax.experimental.pallas import tpu as pltpu
from jax.sharding import PartitionSpec as P

F32 = jnp.float32
BF16 = jnp.bfloat16
MESH = pl.DeviceIdType.MESH

GX, GY = 32, 8
ROUNDS = 8
BINS = 64
ROWS = 512
HI, LO = 32, 128
PAIRS = 16
STEPS = ROWS // (8 * PAIRS)
GROUPS = 8
SMOOTH_SQ = 0.01
FOUR_PI = 4.0 * math.pi


def lookup(rows, index):
    lo, hi = index & (LO - 1), index >> 7
    total = jnp.zeros(index.shape, F32)
    for r, row in enumerate(rows):
        picked = jnp.take_along_axis(jnp.broadcast_to(row, index.shape), lo, axis=1)
        total = jnp.where(hi == r, picked, total)
    return total


def table(ref):
    return [ref[r : r + 1, :] for r in range(HI)]


def stack(x, count):
    return jnp.concatenate([x] * count, axis=0)


def one_hots(index_rows, value_rows):
    bins = lax.broadcasted_iota(jnp.int32, (BINS, 128), 0).astype(F32).astype(BF16)
    zero, one = jnp.zeros((BINS, 128), BF16), jnp.ones((BINS, 128), BF16)
    left, right = [], []
    for index, value in zip(index_rows, value_rows):
        hi = (index >> 7) | ((index & 64) >> 1)
        hi = jnp.broadcast_to(hi.astype(F32), (16, 128)).astype(BF16)
        lo = jnp.broadcast_to((index & 63).astype(F32), (16, 128)).astype(BF16)
        value = jnp.broadcast_to(value, (16, 128))
        upper = value.astype(BF16)
        lower = (value - upper.astype(F32)).astype(BF16)
        at_hi = stack(hi, BINS // 16) == bins
        left.append(
            jnp.concatenate(
                [
                    jnp.where(at_hi, stack(upper, BINS // 16), zero),
                    jnp.where(at_hi, stack(lower, BINS // 16), zero),
                ],
                axis=0,
            )
        )
        right.append(jnp.where(stack(lo, BINS // 16) == bins, one, zero))
    return jnp.concatenate(left, axis=1), jnp.concatenate(right, axis=1)


def scatter_product(index_rows, value_rows):
    left, right = one_hots(index_rows, value_rows)
    return lax.dot_general(left, right, (((1,), (1,)), ((), ())), preferred_element_type=F32)


def as_table(sums):
    bins = sums[0:BINS, :] + sums[BINS : 2 * BINS, :]
    return jnp.concatenate([bins[0:HI, :], bins[HI:BINS, :]], axis=1)


def kernel(
    count_hbm, owner_hbm, nodal_hbm, conn_hbm, matrix_hbm, face_hbm, node_hbm, weight_hbm,
    centroid_hbm, normal_hbm, target_hbm,
    fem_ref, bem_ref,
    count_ref, owner_ref, nodal_ref, conn_ref, matrix_ref, face_ref, node_ref, weight_ref,
    centroid_ref, normal_ref, target_ref,
    halves, gathered, value, total, partial, sent, incoming, spots_out, spots_in, place,
    potential, sums_out, sums_in,
    load_sem, conn_sem, matrix_sem, send_sem, recv_sem, face_send, face_recv, pair_send, pair_recv, entered_sem,
):
    px, py = lax.axis_index("px"), lax.axis_index("py")
    core = px & 1
    sibling = px + 1 - 2 * core
    low_y, high_y = (py + GY - 1) & (GY - 1), (py + 1) & (GY - 1)

    names = ("nodal", "node", "count", "weight", "centroid", "normal", "target", "face", "owner")
    sources = (nodal_hbm, node_hbm, count_hbm, weight_hbm, centroid_hbm, normal_hbm, target_hbm, face_hbm, owner_hbm)
    places = (nodal_ref, node_ref, count_ref, weight_ref, centroid_ref, normal_ref, target_ref, face_ref, owner_ref)
    loads = {
        name: pltpu.make_async_copy(source, where, load_sem.at[i])
        for i, (name, source, where) in enumerate(zip(names, sources, places))
    }

    def conn_load(step):
        rows = pl.ds(pl.multiple_of(step * 8 * PAIRS, 8), 8 * PAIRS)
        return pltpu.make_async_copy(conn_hbm.at[rows], conn_ref.at[rows], conn_sem.at[step])

    def matrix_load(step):
        lanes = pl.ds(pl.multiple_of(step * 256 * PAIRS, 128), 256 * PAIRS)
        return pltpu.make_async_copy(
            matrix_hbm.at[:, lanes], matrix_ref.at[:, lanes], matrix_sem.at[step]
        )

    for name in names:
        loads[name].start()

    @pl.loop(0, STEPS)
    def _(step):
        conn_load(step).start()
        matrix_load(step).start()

    barrier = pltpu.get_barrier_semaphore()

    @pl.loop(1, GX)
    def _(d):
        pl.semaphore_signal(
            barrier, inc=1, device_id=((px + d) & (GX - 1), py), device_id_type=MESH
        )

    even = (py & 1) == 0

    @pl.when(even)
    def _():
        for column in (low_y, high_y):
            pl.semaphore_signal(barrier, inc=1, device_id=(px, column), device_id_type=MESH)

    sublane = lax.broadcasted_iota(jnp.int32, (8, 128), 0)
    lane = lax.broadcasted_iota(jnp.int32, (8, 128), 1)

    loads["nodal"].wait()
    total[...] = jnp.zeros_like(total)
    odd, second, fourth = (sublane & 1) == 1, (sublane & 2) == 2, (sublane & 4) == 4

    def elements(step):
        conn_load(step).wait()
        matrix_load(step).wait()
        base = step * PAIRS
        index_rows, value_rows = [], []
        for u in range(PAIRS):
            at = pl.multiple_of((base + u) * 8, 8)
            nodes = conn_ref[pl.ds(at, 8), :]
            values = lookup(table(nodal_ref), nodes)
            swapped = pltpu.roll(values, 4, 0)
            folded = []
            for chunk in range(2):
                pair = (swapped, values) if chunk == 0 else (values, swapped)
                both = jnp.where(fourth, *pair)
                lanes = pl.ds(pl.multiple_of((base + u) * 256 + 128 * chunk, 128), 128)
                first = matrix_ref[0:8, lanes] * both
                last = matrix_ref[8:16, lanes] * both
                folded.append(
                    jnp.where(second, last + pltpu.roll(last, 2, 0), first + pltpu.roll(first, 6, 0))
                )
            value[8 * u : 8 * u + 8, :] = jnp.where(
                odd, folded[1] + pltpu.roll(folded[1], 1, 0), folded[0] + pltpu.roll(folded[0], 7, 0)
            )
            for chunk in range(2):
                for corner in range(4):
                    index_rows.append(conn_ref[pl.ds(at + 4 * chunk + corner, 1), :])
                    row = 8 * u + (0, 4, 2, 6)[corner] + chunk
                    value_rows.append(value[row : row + 1, :])
        total[...] += scatter_product(index_rows, value_rows)

    pl.loop(0, 2)(elements)

    for name in ("node", "count", "weight", "centroid", "normal", "target"):
        loads[name].wait()
    trace = lookup(table(nodal_ref), stack(node_ref[...], 2))
    live = count_ref[py, px]
    slot = (sublane & 3) * 128 + lane
    weighted = jnp.where(slot < live, stack(weight_ref[...], 2) * trace, 0.0)
    for h in range(2):
        for c in range(3):
            halves[h, 2 * c : 2 * c + 2, :] = centroid_ref[c, 2 * h : 2 * h + 2, :]
            halves[h, 6 + 2 * c : 8 + 2 * c, :] = (
                normal_ref[c, 2 * h : 2 * h + 2, :] * weighted[2 * h : 2 * h + 2, :]
            )

    targets = stack(target_ref[...], 4)
    target_trace = lookup([trace[k : k + 1, :] for k in range(2)], targets)
    for c in range(3):
        where = lookup([centroid_ref[c, k : k + 1, :] for k in range(2)], targets)
        spots_out[2 * c : 2 * c + 2, :] = where[0:2, :]

    pl.semaphore_wait(barrier, GX - 1 + 2 * (py & 1))

    @pl.when(jnp.logical_not(even))
    def _():
        for column in (low_y, high_y):
            pl.semaphore_signal(entered_sem, inc=1, device_id=(px, column), device_id_type=MESH)

    def to_other(d, source):
        target = (px + d) & (GX - 1)
        return pltpu.make_async_remote_copy(
            src_ref=halves.at[target & 1],
            dst_ref=gathered.at[source],
            send_sem=send_sem.at[d],
            recv_sem=recv_sem.at[source],
            device_id=(target, py),
            device_id_type=MESH,
        )

    def to_sibling(source, where, n):
        return pltpu.make_async_remote_copy(
            src_ref=source,
            dst_ref=where,
            send_sem=pair_send.at[n],
            recv_sem=pair_recv.at[n],
            device_id=(sibling, py),
            device_id_type=MESH,
        )

    send_spots = to_sibling(spots_out, spots_in, 0)
    send_sums = to_sibling(sums_out, sums_in, 1)

    @pl.loop(1, GX)
    def _(d):
        to_other(d, px).start()

    send_spots.start()
    gathered[px] = halves[core]

    def spread(ref, first):
        for c in range(3):
            for half in range(2):
                row = ref[2 * c + half : 2 * c + half + 1, :]
                rows = slice(first + 128 * half, first + 128 * half + 128)
                place[c, rows, :] = jnp.broadcast_to(row, (128, 128)).T

    pl.loop(2, STEPS)(elements)

    partial[...] = as_table(total[...])

    loads["face"].wait()
    outgoing = lookup(table(partial), face_ref[...])
    for f in range(4):
        for half in range(2):
            sent[f, half : half + 1, :] = outgoing[4 * half + f : 4 * half + f + 1, :]
    neighbours = (
        ((px + GX - 1) & (GX - 1), py),
        ((px + 1) & (GX - 1), py),
        (px, low_y),
        (px, high_y),
    )
    faces = [
        pltpu.make_async_remote_copy(
            src_ref=sent.at[f],
            dst_ref=incoming.at[f ^ 1],
            send_sem=face_send.at[f],
            recv_sem=face_recv.at[f ^ 1],
            device_id=neighbours[f],
            device_id_type=MESH,
        )
        for f in range(4)
    ]
    for face in faces[0:2]:
        face.start()

    @pl.when(even)
    def _():
        pl.semaphore_wait(entered_sem, 2)

    for face in faces[2:4]:
        face.start()

    loads["owner"].wait()
    spread(spots_out, 256)
    send_spots.wait_recv()
    spread(spots_in, 0)

    @pl.loop(1, GX)
    def _(d):
        to_other(d, (px + GX - d) & (GX - 1)).wait_recv()

    def double_layer(first):
        @pl.loop(0, 32 // GROUPS)
        def _(part):
            at = [pl.multiple_of(8 * (GROUPS * part + g), 8) for g in range(GROUPS)]
            spots = [[place[c, pl.ds(first + at[g], 8), :] for c in range(3)] for g in range(GROUPS)]

            def one_round(r, sums):
                owner = owner_ref[r]
                sums = list(sums)
                for k in range(2):
                    rows = [
                        jnp.broadcast_to(gathered[owner, 2 * c + k : 2 * c + k + 1, :], (8, 128))
                        for c in range(6)
                    ]
                    for g in range(GROUPS):
                        dx, dy, dz = (spots[g][c] - rows[c] for c in range(3))
                        inverse = lax.rsqrt(dx * dx + dy * dy + dz * dz + SMOOTH_SQ)
                        along = rows[3] * dx + rows[4] * dy + rows[5] * dz
                        sums[g] = sums[g] + along * (inverse * inverse * inverse)
                return tuple(sums)

            sums = lax.fori_loop(
                0, ROUNDS, one_round, (jnp.zeros((8, 128), F32),) * GROUPS, unroll=2
            )
            for g in range(GROUPS):
                potential[pl.ds(at[g], 8), :] = sums[g]

        return [
            jnp.sum(potential[128 * half : 128 * half + 128, :].T, axis=0, keepdims=True)
            for half in range(2)
        ]

    for half, row in enumerate(double_layer(0)):
        sums_out[half : half + 1, :] = row
    send_sums.start()
    own = double_layer(256)
    send_sums.wait_recv()
    for half in range(2):
        bem_ref[half : half + 1, :] = (
            own[half] + sums_in[half : half + 1, :]
        ) * (1.0 / FOUR_PI) - 0.5 * target_trace[half : half + 1, :]

    send_spots.wait_send()
    send_sums.wait_send()

    @pl.loop(1, GX)
    def _(d):
        to_other(d, px).wait_send()

    for face in faces:
        face.wait_send()
    for face in faces:
        face.wait_recv()
    present = (px > 0, px < GX - 1, py > 0, py < GY - 1)
    index_rows, value_rows = [], []
    for f in range(4):
        for half in range(2):
            row = 4 * half + f
            index_rows.append(face_ref[row : row + 1, :])
            value_rows.append(jnp.where(present[f], incoming[f, half : half + 1, :], 0.0))
    fem_ref[...] = partial[...] + as_table(scatter_product(index_rows, value_rows))


def per_device(
    nodal_field, element_matrix, connectivity, face_nodes, panel_node, panel_weight,
    centroid, panel_normal, panel_count, target_index, round_owner,
):
    vmem = pl.BlockSpec(memory_space=pltpu.VMEM)
    hbm = pl.BlockSpec(memory_space=pl.ANY)
    i32 = jnp.int32
    connect = connectivity[0, 0].reshape(4, 128, 128).transpose(1, 0, 2).reshape(ROWS, 128)
    faces = face_nodes[0, 0].reshape(4, 2, 128).transpose(1, 0, 2).reshape(8, 128)
    fem, bem = pl.pallas_call(
        kernel,
        out_shape=(
            pltpu.VMEM((HI, LO), F32),
            pltpu.VMEM((2, 128), F32),
        ),
        in_specs=[hbm] * 11,
        out_specs=(vmem, vmem),
        scratch_shapes=[
            pltpu.SMEM((GY, GX), i32),
            pltpu.SMEM((ROUNDS,), i32),
            pltpu.VMEM((HI, LO), F32),
            pltpu.VMEM((ROWS, 128), i32),
            pltpu.VMEM((16, ROWS * 32), F32),
            pltpu.VMEM((8, 128), i32),
            pltpu.VMEM((4, 128), i32),
            pltpu.VMEM((4, 128), F32),
            pltpu.VMEM((3, 4, 128), F32),
            pltpu.VMEM((3, 4, 128), F32),
            pltpu.VMEM((2, 128), i32),
            pltpu.VMEM((2, 12, 128), F32),
            pltpu.VMEM((GX, 12, 128), F32),
            pltpu.VMEM((8 * PAIRS, 128), F32),
            pltpu.VMEM((2 * BINS, BINS), F32),
            pltpu.VMEM((HI, LO), F32),
            pltpu.VMEM((4, 2, 128), F32),
            pltpu.VMEM((4, 2, 128), F32),
            pltpu.VMEM((6, 128), F32),
            pltpu.VMEM((6, 128), F32),
            pltpu.VMEM((3, 512, 128), F32),
            pltpu.VMEM((256, 128), F32),
            pltpu.VMEM((2, 128), F32),
            pltpu.VMEM((2, 128), F32),
            pltpu.SemaphoreType.DMA((9,)),
            pltpu.SemaphoreType.DMA((STEPS,)),
            pltpu.SemaphoreType.DMA((STEPS,)),
            pltpu.SemaphoreType.DMA((GX,)),
            pltpu.SemaphoreType.DMA((GX,)),
            pltpu.SemaphoreType.DMA((4,)),
            pltpu.SemaphoreType.DMA((4,)),
            pltpu.SemaphoreType.DMA((2,)),
            pltpu.SemaphoreType.DMA((2,)),
            pltpu.SemaphoreType.REGULAR,
        ],
        compiler_params=pltpu.CompilerParams(
            collective_id=0, has_side_effects=True, vmem_limit_bytes=60 * 1024 * 1024
        ),
        name="apply",
    )(
        panel_count.T,
        round_owner,
        nodal_field.reshape(HI, LO),
        connect,
        element_matrix.reshape(16, -1),
        faces,
        panel_node.reshape(4, 128),
        panel_weight.reshape(4, 128),
        centroid.transpose(0, 2, 1, 3).reshape(3, 4, 128),
        panel_normal.transpose(0, 2, 1, 3).reshape(3, 4, 128),
        target_index.reshape(2, 128),
    )
    return fem.reshape(1, 1, HI * LO), bem.reshape(1, 1, 256)


def solution(mesh):
    split = P("px", "py")
    return jax.shard_map(
        per_device,
        mesh=mesh,
        in_specs=(split,) * 8 + (P(), split, P()),
        out_specs=(split, split),
        check_vma=False,
    )
```

```python
import functools
import math

import jax
import jax.numpy as jnp
from jax import lax
from jax.experimental import pallas as pl
from jax.experimental.pallas import tpu as pltpu
from jax.sharding import PartitionSpec as P

F32 = jnp.float32
BF16 = jnp.bfloat16
MESH = pl.DeviceIdType.MESH

GX, GY = 32, 8
ROUNDS = 8
BINS = 64
ROWS = 512
HI, LO = 32, 128
PAIRS = 16
STEPS = ROWS // (8 * PAIRS)
GROUPS = 8
SMOOTH_SQ = 0.01
FOUR_PI = 4.0 * math.pi


def lookup(rows, index):
    lo, hi = index & (LO - 1), index >> 7
    total = jnp.zeros(index.shape, F32)
    for r, row in enumerate(rows):
        picked = jnp.take_along_axis(jnp.broadcast_to(row, index.shape), lo, axis=1)
        total = jnp.where(hi == r, picked, total)
    return total


def table(ref):
    return [ref[r : r + 1, :] for r in range(HI)]


def stack(x, count):
    return jnp.concatenate([x] * count, axis=0)


def one_hots(index_rows, value_rows):
    bins = lax.broadcasted_iota(jnp.int32, (BINS, 128), 0).astype(F32).astype(BF16)
    zero, one = jnp.zeros((BINS, 128), BF16), jnp.ones((BINS, 128), BF16)
    left, right = [], []
    for index, value in zip(index_rows, value_rows):
        hi = (index >> 7) | ((index & 64) >> 1)
        hi = jnp.broadcast_to(hi.astype(F32), (16, 128)).astype(BF16)
        lo = jnp.broadcast_to((index & 63).astype(F32), (16, 128)).astype(BF16)
        value = jnp.broadcast_to(value, (16, 128))
        upper = value.astype(BF16)
        lower = (value - upper.astype(F32)).astype(BF16)
        at_hi = stack(hi, BINS // 16) == bins
        left.append(
            jnp.concatenate(
                [
                    jnp.where(at_hi, stack(upper, BINS // 16), zero),
                    jnp.where(at_hi, stack(lower, BINS // 16), zero),
                ],
                axis=0,
            )
        )
        right.append(jnp.where(stack(lo, BINS // 16) == bins, one, zero))
    return jnp.concatenate(left, axis=1), jnp.concatenate(right, axis=1)


def scatter_product(index_rows, value_rows):
    left, right = one_hots(index_rows, value_rows)
    return lax.dot_general(left, right, (((1,), (1,)), ((), ())), preferred_element_type=F32)


def as_table(sums):
    bins = sums[0:BINS, :] + sums[BINS : 2 * BINS, :]
    return jnp.concatenate([bins[0:HI, :], bins[HI:BINS, :]], axis=1)


def kernel(
    count_hbm, owner_hbm, nodal_hbm, conn_hbm, matrix_hbm, face_hbm, node_hbm, weight_hbm,
    centroid_hbm, normal_hbm, target_hbm,
    fem_ref, bem_ref,
    count_ref, owner_ref, nodal_ref, conn_ref, matrix_ref, face_ref, node_ref, weight_ref,
    centroid_ref, normal_ref, target_ref,
    halves, gathered, value, total, partial, sent, incoming, spots_out, spots_in, place,
    potential, sums_out, sums_in,
    load_sem, conn_sem, matrix_sem, send_sem, recv_sem, face_send, face_recv, pair_send, pair_recv, entered_sem,
):
    px, py = lax.axis_index("px"), lax.axis_index("py")
    core = px & 1
    sibling = px + 1 - 2 * core
    low_y, high_y = (py + GY - 1) & (GY - 1), (py + 1) & (GY - 1)

    names = ("nodal", "node", "count", "weight", "centroid", "normal", "target", "face", "owner")
    sources = (nodal_hbm, node_hbm, count_hbm, weight_hbm, centroid_hbm, normal_hbm, target_hbm, face_hbm, owner_hbm)
    places = (nodal_ref, node_ref, count_ref, weight_ref, centroid_ref, normal_ref, target_ref, face_ref, owner_ref)
    loads = {
        name: pltpu.make_async_copy(source, where, load_sem.at[i])
        for i, (name, source, where) in enumerate(zip(names, sources, places))
    }

    def conn_load(step):
        rows = pl.ds(pl.multiple_of(step * 8 * PAIRS, 8), 8 * PAIRS)
        return pltpu.make_async_copy(conn_hbm.at[rows], conn_ref.at[rows], conn_sem.at[step])

    def matrix_load(step):
        lanes = pl.ds(pl.multiple_of(step * 256 * PAIRS, 128), 256 * PAIRS)
        return pltpu.make_async_copy(
            matrix_hbm.at[:, lanes], matrix_ref.at[:, lanes], matrix_sem.at[step]
        )

    for name in names:
        loads[name].start()

    @pl.loop(0, STEPS)
    def _(step):
        conn_load(step).start()
        matrix_load(step).start()

    barrier = pltpu.get_barrier_semaphore()

    @pl.loop(1, GX)
    def _(d):
        pl.semaphore_signal(
            barrier, inc=1, device_id=((px + d) & (GX - 1), py), device_id_type=MESH
        )

    even = (py & 1) == 0

    @pl.when(even)
    def _():
        for column in (low_y, high_y):
            pl.semaphore_signal(barrier, inc=1, device_id=(px, column), device_id_type=MESH)

    sublane = lax.broadcasted_iota(jnp.int32, (8, 128), 0)
    lane = lax.broadcasted_iota(jnp.int32, (8, 128), 1)

    loads["nodal"].wait()
    for name in ("node", "count", "weight", "centroid", "normal", "target"):
        loads[name].wait()
    trace = lookup(table(nodal_ref), stack(node_ref[...], 2))
    live = count_ref[py, px]
    slot = (sublane & 3) * 128 + lane
    weighted = jnp.where(slot < live, stack(weight_ref[...], 2) * trace, 0.0)
    for h in range(2):
        for c in range(3):
            halves[h, 2 * c : 2 * c + 2, :] = centroid_ref[c, 2 * h : 2 * h + 2, :]
            halves[h, 6 + 2 * c : 8 + 2 * c, :] = (
                normal_ref[c, 2 * h : 2 * h + 2, :] * weighted[2 * h : 2 * h + 2, :]
            )

    targets = stack(target_ref[...], 4)
    target_trace = lookup([trace[k : k + 1, :] for k in range(2)], targets)
    for c in range(3):
        where = lookup([centroid_ref[c, k : k + 1, :] for k in range(2)], targets)
        spots_out[2 * c : 2 * c + 2, :] = where[0:2, :]

    total[...] = jnp.zeros_like(total)
    odd, second, fourth = (sublane & 1) == 1, (sublane & 2) == 2, (sublane & 4) == 4

    def elements(step):
        conn_load(step).wait()
        matrix_load(step).wait()
        base = step * PAIRS
        index_rows, value_rows = [], []
        for u in range(PAIRS):
            at = pl.multiple_of((base + u) * 8, 8)
            nodes = conn_ref[pl.ds(at, 8), :]
            values = lookup(table(nodal_ref), nodes)
            swapped = pltpu.roll(values, 4, 0)
            folded = []
            for chunk in range(2):
                pair = (swapped, values) if chunk == 0 else (values, swapped)
                both = jnp.where(fourth, *pair)
                lanes = pl.ds(pl.multiple_of((base + u) * 256 + 128 * chunk, 128), 128)
                first = matrix_ref[0:8, lanes] * both
                last = matrix_ref[8:16, lanes] * both
                folded.append(
                    jnp.where(second, last + pltpu.roll(last, 2, 0), first + pltpu.roll(first, 6, 0))
                )
            value[8 * u : 8 * u + 8, :] = jnp.where(
                odd, folded[1] + pltpu.roll(folded[1], 1, 0), folded[0] + pltpu.roll(folded[0], 7, 0)
            )
            for chunk in range(2):
                for corner in range(4):
                    index_rows.append(conn_ref[pl.ds(at + 4 * chunk + corner, 1), :])
                    row = 8 * u + (0, 4, 2, 6)[corner] + chunk
                    value_rows.append(value[row : row + 1, :])
        total[...] += scatter_product(index_rows, value_rows)

    ahead = 1 + 2 * (py & 1)
    pl.loop(0, ahead)(elements)

    pl.semaphore_wait(barrier, GX - 1 + 2 * (py & 1))

    @pl.when(jnp.logical_not(even))
    def _():
        for column in (low_y, high_y):
            pl.semaphore_signal(entered_sem, inc=1, device_id=(px, column), device_id_type=MESH)

    def to_other(d, source):
        target = (px + d) & (GX - 1)
        return pltpu.make_async_remote_copy(
            src_ref=halves.at[target & 1],
            dst_ref=gathered.at[source],
            send_sem=send_sem.at[d],
            recv_sem=recv_sem.at[source],
            device_id=(target, py),
            device_id_type=MESH,
        )

    def to_sibling(source, where, n):
        return pltpu.make_async_remote_copy(
            src_ref=source,
            dst_ref=where,
            send_sem=pair_send.at[n],
            recv_sem=pair_recv.at[n],
            device_id=(sibling, py),
            device_id_type=MESH,
        )

    send_spots = to_sibling(spots_out, spots_in, 0)
    send_sums = to_sibling(sums_out, sums_in, 1)

    @pl.loop(1, GX)
    def _(d):
        to_other(d, px).start()

    send_spots.start()
    gathered[px] = halves[core]

    def spread(ref, first):
        for c in range(3):
            for half in range(2):
                row = ref[2 * c + half : 2 * c + half + 1, :]
                rows = slice(first + 128 * half, first + 128 * half + 128)
                place[c, rows, :] = jnp.broadcast_to(row, (128, 128)).T

    pl.loop(ahead, STEPS)(elements)

    partial[...] = as_table(total[...])

    loads["face"].wait()
    outgoing = lookup(table(partial), face_ref[...])
    for f in range(4):
        for half in range(2):
            sent[f, half : half + 1, :] = outgoing[4 * half + f : 4 * half + f + 1, :]
    neighbours = (
        ((px + GX - 1) & (GX - 1), py),
        ((px + 1) & (GX - 1), py),
        (px, low_y),
        (px, high_y),
    )
    faces = [
        pltpu.make_async_remote_copy(
            src_ref=sent.at[f],
            dst_ref=incoming.at[f ^ 1],
            send_sem=face_send.at[f],
            recv_sem=face_recv.at[f ^ 1],
            device_id=neighbours[f],
            device_id_type=MESH,
        )
        for f in range(4)
    ]
    for face in faces[0:2]:
        face.start()

    @pl.when(jnp.logical_not(even))
    def _():
        for face in faces[2:4]:
            face.start()

    loads["owner"].wait()
    spread(spots_out, 256)
    send_spots.wait_recv()
    spread(spots_in, 0)

    @pl.loop(1, GX)
    def _(d):
        to_other(d, px).wait_send()

    @pl.loop(1, GX)
    def _(d):
        to_other(d, (px + GX - d) & (GX - 1)).wait_recv()

    def double_layer(first):
        @pl.loop(0, 32 // GROUPS)
        def _(part):
            at = [pl.multiple_of(8 * (GROUPS * part + g), 8) for g in range(GROUPS)]
            spots = [[place[c, pl.ds(first + at[g], 8), :] for c in range(3)] for g in range(GROUPS)]

            def one_round(r, sums):
                owner = owner_ref[r]
                sums = list(sums)
                for k in range(2):
                    rows = [
                        jnp.broadcast_to(gathered[owner, 2 * c + k : 2 * c + k + 1, :], (8, 128))
                        for c in range(6)
                    ]
                    for g in range(GROUPS):
                        dx, dy, dz = (spots[g][c] - rows[c] for c in range(3))
                        inverse = lax.rsqrt(dx * dx + dy * dy + dz * dz + SMOOTH_SQ)
                        along = rows[3] * dx + rows[4] * dy + rows[5] * dz
                        sums[g] = sums[g] + along * (inverse * inverse * inverse)
                return tuple(sums)

            sums = lax.fori_loop(
                0, ROUNDS, one_round, (jnp.zeros((8, 128), F32),) * GROUPS, unroll=2
            )
            for g in range(GROUPS):
                potential[pl.ds(at[g], 8), :] = sums[g]

        return [
            jnp.sum(potential[128 * half : 128 * half + 128, :].T, axis=0, keepdims=True)
            for half in range(2)
        ]

    for half, row in enumerate(double_layer(0)):
        sums_out[half : half + 1, :] = row
    send_sums.start()

    @pl.when(even)
    def _():
        pl.semaphore_wait(entered_sem, 2)
        for face in faces[2:4]:
            face.start()

    own = double_layer(256)
    send_sums.wait_recv()
    for half in range(2):
        bem_ref[half : half + 1, :] = (
            own[half] + sums_in[half : half + 1, :]
        ) * (1.0 / FOUR_PI) - 0.5 * target_trace[half : half + 1, :]

    send_spots.wait_send()
    send_sums.wait_send()

    for face in faces:
        face.wait_send()
    for face in faces:
        face.wait_recv()
    present = (px > 0, px < GX - 1, py > 0, py < GY - 1)
    index_rows, value_rows = [], []
    for f in range(4):
        for half in range(2):
            row = 4 * half + f
            index_rows.append(face_ref[row : row + 1, :])
            value_rows.append(jnp.where(present[f], incoming[f, half : half + 1, :], 0.0))
    fem_ref[...] = partial[...] + as_table(scatter_product(index_rows, value_rows))


def per_device(
    nodal_field, element_matrix, connectivity, face_nodes, panel_node, panel_weight,
    centroid, panel_normal, panel_count, target_index, round_owner,
):
    vmem = pl.BlockSpec(memory_space=pltpu.VMEM)
    hbm = pl.BlockSpec(memory_space=pl.ANY)
    i32 = jnp.int32
    connect = connectivity[0, 0].reshape(4, 128, 128).transpose(1, 0, 2).reshape(ROWS, 128)
    faces = face_nodes[0, 0].reshape(4, 2, 128).transpose(1, 0, 2).reshape(8, 128)
    fem, bem = pl.pallas_call(
        kernel,
        out_shape=(
            pltpu.VMEM((HI, LO), F32),
            pltpu.VMEM((2, 128), F32),
        ),
        in_specs=[hbm] * 11,
        out_specs=(vmem, vmem),
        scratch_shapes=[
            pltpu.SMEM((GY, GX), i32),
            pltpu.SMEM((ROUNDS,), i32),
            pltpu.VMEM((HI, LO), F32),
            pltpu.VMEM((ROWS, 128), i32),
            pltpu.VMEM((16, ROWS * 32), F32),
            pltpu.VMEM((8, 128), i32),
            pltpu.VMEM((4, 128), i32),
            pltpu.VMEM((4, 128), F32),
            pltpu.VMEM((3, 4, 128), F32),
            pltpu.VMEM((3, 4, 128), F32),
            pltpu.VMEM((2, 128), i32),
            pltpu.VMEM((2, 12, 128), F32),
            pltpu.VMEM((GX, 12, 128), F32),
            pltpu.VMEM((8 * PAIRS, 128), F32),
            pltpu.VMEM((2 * BINS, BINS), F32),
            pltpu.VMEM((HI, LO), F32),
            pltpu.VMEM((4, 2, 128), F32),
            pltpu.VMEM((4, 2, 128), F32),
            pltpu.VMEM((6, 128), F32),
            pltpu.VMEM((6, 128), F32),
            pltpu.VMEM((3, 512, 128), F32),
            pltpu.VMEM((256, 128), F32),
            pltpu.VMEM((2, 128), F32),
            pltpu.VMEM((2, 128), F32),
            pltpu.SemaphoreType.DMA((9,)),
            pltpu.SemaphoreType.DMA((STEPS,)),
            pltpu.SemaphoreType.DMA((STEPS,)),
            pltpu.SemaphoreType.DMA((GX,)),
            pltpu.SemaphoreType.DMA((GX,)),
            pltpu.SemaphoreType.DMA((4,)),
            pltpu.SemaphoreType.DMA((4,)),
            pltpu.SemaphoreType.DMA((2,)),
            pltpu.SemaphoreType.DMA((2,)),
            pltpu.SemaphoreType.REGULAR,
        ],
        compiler_params=pltpu.CompilerParams(
            collective_id=0, has_side_effects=True, vmem_limit_bytes=60 * 1024 * 1024
        ),
        name="apply",
    )(
        panel_count.T,
        round_owner,
        nodal_field.reshape(HI, LO),
        connect,
        element_matrix.reshape(16, -1),
        faces,
        panel_node.reshape(4, 128),
        panel_weight.reshape(4, 128),
        centroid.transpose(0, 2, 1, 3).reshape(3, 4, 128),
        panel_normal.transpose(0, 2, 1, 3).reshape(3, 4, 128),
        target_index.reshape(2, 128),
    )
    return fem.reshape(1, 1, HI * LO), bem.reshape(1, 1, 256)


def solution(mesh):
    split = P("px", "py")
    return jax.shard_map(
        per_device,
        mesh=mesh,
        in_specs=(split,) * 8 + (P(), split, P()),
        out_specs=(split, split),
        check_vma=False,
    )
```

```python
import functools
import math

import jax
import jax.numpy as jnp
from jax import lax
from jax.experimental import pallas as pl
from jax.experimental.pallas import tpu as pltpu
from jax.sharding import PartitionSpec as P

F32 = jnp.float32
BF16 = jnp.bfloat16
MESH = pl.DeviceIdType.MESH

GX, GY = 32, 8
ROUNDS = 8
BINS = 64
ROWS = 512
HI, LO = 32, 128
PAIRS = 16
STEPS = ROWS // (8 * PAIRS)
GROUPS = 8
SMOOTH_SQ = 0.01
FOUR_PI = 4.0 * math.pi


def lookup(rows, index):
    lo, hi = index & (LO - 1), index >> 7
    total = jnp.zeros(index.shape, F32)
    for r, row in enumerate(rows):
        picked = jnp.take_along_axis(jnp.broadcast_to(row, index.shape), lo, axis=1)
        total = jnp.where(hi == r, picked, total)
    return total


def table(ref):
    return [ref[r : r + 1, :] for r in range(HI)]


def stack(x, count):
    return jnp.concatenate([x] * count, axis=0)


def one_hots(index_rows, value_rows):
    bins = lax.broadcasted_iota(jnp.int32, (BINS, 128), 0).astype(F32).astype(BF16)
    zero, one = jnp.zeros((BINS, 128), BF16), jnp.ones((BINS, 128), BF16)
    left, right = [], []
    for index, value in zip(index_rows, value_rows):
        hi = (index >> 7) | ((index & 64) >> 1)
        hi = jnp.broadcast_to(hi.astype(F32), (16, 128)).astype(BF16)
        lo = jnp.broadcast_to((index & 63).astype(F32), (16, 128)).astype(BF16)
        value = jnp.broadcast_to(value, (16, 128))
        upper = value.astype(BF16)
        lower = (value - upper.astype(F32)).astype(BF16)
        at_hi = stack(hi, BINS // 16) == bins
        left.append(
            jnp.concatenate(
                [
                    jnp.where(at_hi, stack(upper, BINS // 16), zero),
                    jnp.where(at_hi, stack(lower, BINS // 16), zero),
                ],
                axis=0,
            )
        )
        right.append(jnp.where(stack(lo, BINS // 16) == bins, one, zero))
    return jnp.concatenate(left, axis=1), jnp.concatenate(right, axis=1)


def scatter_product(index_rows, value_rows):
    left, right = one_hots(index_rows, value_rows)
    return lax.dot_general(left, right, (((1,), (1,)), ((), ())), preferred_element_type=F32)


def as_table(sums):
    bins = sums[0:BINS, :] + sums[BINS : 2 * BINS, :]
    return jnp.concatenate([bins[0:HI, :], bins[HI:BINS, :]], axis=1)


def kernel(
    count_hbm, owner_hbm, nodal_hbm, conn_hbm, matrix_hbm, face_hbm, node_hbm, weight_hbm,
    centroid_hbm, normal_hbm, target_hbm,
    fem_ref, bem_ref,
    count_ref, owner_ref, nodal_ref, conn_ref, matrix_ref, face_ref, node_ref, weight_ref,
    centroid_ref, normal_ref, target_ref,
    halves, gathered, value, total, partial, sent, incoming, spots_out, spots_in, place,
    potential, sums_out, sums_in,
    load_sem, conn_sem, matrix_sem, send_sem, recv_sem, face_send, face_recv, pair_send, pair_recv, entered_sem,
):
    px, py = lax.axis_index("px"), lax.axis_index("py")
    core = px & 1
    sibling = px + 1 - 2 * core
    low_y, high_y = (py + GY - 1) & (GY - 1), (py + 1) & (GY - 1)

    names = ("nodal", "node", "count", "weight", "centroid", "normal", "target", "face", "owner")
    sources = (nodal_hbm, node_hbm, count_hbm, weight_hbm, centroid_hbm, normal_hbm, target_hbm, face_hbm, owner_hbm)
    places = (nodal_ref, node_ref, count_ref, weight_ref, centroid_ref, normal_ref, target_ref, face_ref, owner_ref)
    loads = {
        name: pltpu.make_async_copy(source, where, load_sem.at[i])
        for i, (name, source, where) in enumerate(zip(names, sources, places))
    }

    def conn_load(step):
        rows = pl.ds(pl.multiple_of(step * 8 * PAIRS, 8), 8 * PAIRS)
        return pltpu.make_async_copy(conn_hbm.at[rows], conn_ref.at[rows], conn_sem.at[step])

    def matrix_load(step):
        lanes = pl.ds(pl.multiple_of(step * 256 * PAIRS, 128), 256 * PAIRS)
        return pltpu.make_async_copy(
            matrix_hbm.at[:, lanes], matrix_ref.at[:, lanes], matrix_sem.at[step]
        )

    for name in names:
        loads[name].start()

    @pl.loop(0, STEPS)
    def _(step):
        conn_load(step).start()
        matrix_load(step).start()

    barrier = pltpu.get_barrier_semaphore()

    @pl.loop(1, GX)
    def _(d):
        pl.semaphore_signal(
            barrier, inc=1, device_id=((px + d) & (GX - 1), py), device_id_type=MESH
        )

    even = (py & 1) == 0
    late = jnp.logical_not(even)
    present = (px > 0, px < GX - 1, py > 0, py < GY - 1)
    columns = present[2].astype(jnp.int32) + present[3].astype(jnp.int32)

    def greet(semaphore, ours):
        for column, there in ((low_y, present[2]), (high_y, present[3])):

            @pl.when(jnp.logical_and(ours, there))
            def _():
                pl.semaphore_signal(
                    semaphore, inc=1, device_id=(px, column), device_id_type=MESH
                )

    greet(barrier, even)

    sublane = lax.broadcasted_iota(jnp.int32, (8, 128), 0)
    lane = lax.broadcasted_iota(jnp.int32, (8, 128), 1)

    loads["nodal"].wait()
    for name in ("node", "count", "weight", "centroid", "normal", "target"):
        loads[name].wait()
    trace = lookup(table(nodal_ref), stack(node_ref[...], 2))
    live = count_ref[py, px]
    slot = (sublane & 3) * 128 + lane
    weighted = jnp.where(slot < live, stack(weight_ref[...], 2) * trace, 0.0)
    for h in range(2):
        for c in range(3):
            halves[h, 2 * c : 2 * c + 2, :] = centroid_ref[c, 2 * h : 2 * h + 2, :]
            halves[h, 6 + 2 * c : 8 + 2 * c, :] = (
                normal_ref[c, 2 * h : 2 * h + 2, :] * weighted[2 * h : 2 * h + 2, :]
            )

    targets = stack(target_ref[...], 4)
    target_trace = lookup([trace[k : k + 1, :] for k in range(2)], targets)
    for c in range(3):
        where = lookup([centroid_ref[c, k : k + 1, :] for k in range(2)], targets)
        spots_out[2 * c : 2 * c + 2, :] = where[0:2, :]

    total[...] = jnp.zeros_like(total)
    odd, second, fourth = (sublane & 1) == 1, (sublane & 2) == 2, (sublane & 4) == 4

    def elements(step):
        conn_load(step).wait()
        matrix_load(step).wait()
        base = step * PAIRS
        index_rows, value_rows = [], []
        for u in range(PAIRS):
            at = pl.multiple_of((base + u) * 8, 8)
            nodes = conn_ref[pl.ds(at, 8), :]
            values = lookup(table(nodal_ref), nodes)
            swapped = pltpu.roll(values, 4, 0)
            folded = []
            for chunk in range(2):
                pair = (swapped, values) if chunk == 0 else (values, swapped)
                both = jnp.where(fourth, *pair)
                lanes = pl.ds(pl.multiple_of((base + u) * 256 + 128 * chunk, 128), 128)
                first = matrix_ref[0:8, lanes] * both
                last = matrix_ref[8:16, lanes] * both
                folded.append(
                    jnp.where(second, last + pltpu.roll(last, 2, 0), first + pltpu.roll(first, 6, 0))
                )
            value[8 * u : 8 * u + 8, :] = jnp.where(
                odd, folded[1] + pltpu.roll(folded[1], 1, 0), folded[0] + pltpu.roll(folded[0], 7, 0)
            )
            for chunk in range(2):
                for corner in range(4):
                    index_rows.append(conn_ref[pl.ds(at + 4 * chunk + corner, 1), :])
                    row = 8 * u + (0, 4, 2, 6)[corner] + chunk
                    value_rows.append(value[row : row + 1, :])
        total[...] += scatter_product(index_rows, value_rows)

    ahead = 1 + 2 * (py & 1)
    pl.loop(0, ahead)(elements)

    pl.semaphore_wait(barrier, GX - 1 + columns * (py & 1))
    greet(entered_sem, late)

    def to_other(d, source):
        target = (px + d) & (GX - 1)
        return pltpu.make_async_remote_copy(
            src_ref=halves.at[target & 1],
            dst_ref=gathered.at[source],
            send_sem=send_sem.at[d],
            recv_sem=recv_sem.at[source],
            device_id=(target, py),
            device_id_type=MESH,
        )

    def to_sibling(source, where, n):
        return pltpu.make_async_remote_copy(
            src_ref=source,
            dst_ref=where,
            send_sem=pair_send.at[n],
            recv_sem=pair_recv.at[n],
            device_id=(sibling, py),
            device_id_type=MESH,
        )

    send_spots = to_sibling(spots_out, spots_in, 0)
    send_sums = to_sibling(sums_out, sums_in, 1)

    @pl.loop(1, GX)
    def _(d):
        to_other(d, px).start()

    send_spots.start()
    gathered[px] = halves[core]

    def spread(ref, first):
        for c in range(3):
            for half in range(2):
                row = ref[2 * c + half : 2 * c + half + 1, :]
                rows = slice(first + 128 * half, first + 128 * half + 128)
                place[c, rows, :] = jnp.broadcast_to(row, (128, 128)).T

    pl.loop(ahead, STEPS)(elements)

    partial[...] = as_table(total[...])

    loads["face"].wait()
    outgoing = lookup(table(partial), face_ref[...])
    for f in range(4):
        for half in range(2):
            sent[f, half : half + 1, :] = outgoing[4 * half + f : 4 * half + f + 1, :]
    neighbours = (
        ((px + GX - 1) & (GX - 1), py),
        ((px + 1) & (GX - 1), py),
        (px, low_y),
        (px, high_y),
    )
    faces = [
        pltpu.make_async_remote_copy(
            src_ref=sent.at[f],
            dst_ref=incoming.at[f ^ 1],
            send_sem=face_send.at[f],
            recv_sem=face_recv.at[f ^ 1],
            device_id=neighbours[f],
            device_id_type=MESH,
        )
        for f in range(4)
    ]
    for f in range(2):
        pl.when(present[f])(faces[f].start)
    for f in range(2, 4):
        pl.when(jnp.logical_and(late, present[f]))(faces[f].start)

    loads["owner"].wait()
    spread(spots_out, 256)
    send_spots.wait_recv()
    spread(spots_in, 0)

    @pl.loop(1, GX)
    def _(d):
        to_other(d, px).wait_send()

    @pl.loop(1, GX)
    def _(d):
        to_other(d, (px + GX - d) & (GX - 1)).wait_recv()

    def double_layer(first):
        @pl.loop(0, 32 // GROUPS)
        def _(part):
            at = [pl.multiple_of(8 * (GROUPS * part + g), 8) for g in range(GROUPS)]
            spots = [[place[c, pl.ds(first + at[g], 8), :] for c in range(3)] for g in range(GROUPS)]

            def one_round(r, sums):
                owner = owner_ref[r]
                sums = list(sums)
                for k in range(2):
                    rows = [
                        jnp.broadcast_to(gathered[owner, 2 * c + k : 2 * c + k + 1, :], (8, 128))
                        for c in range(6)
                    ]
                    for g in range(GROUPS):
                        dx, dy, dz = (spots[g][c] - rows[c] for c in range(3))
                        inverse = lax.rsqrt(dx * dx + dy * dy + dz * dz + SMOOTH_SQ)
                        along = rows[3] * dx + rows[4] * dy + rows[5] * dz
                        sums[g] = sums[g] + along * (inverse * inverse * inverse)
                return tuple(sums)

            sums = lax.fori_loop(
                0, ROUNDS, one_round, (jnp.zeros((8, 128), F32),) * GROUPS, unroll=2
            )
            for g in range(GROUPS):
                potential[pl.ds(at[g], 8), :] = sums[g]

        return [
            jnp.sum(potential[128 * half : 128 * half + 128, :].T, axis=0, keepdims=True)
            for half in range(2)
        ]

    for half, row in enumerate(double_layer(0)):
        sums_out[half : half + 1, :] = row
    send_sums.start()

    @pl.when(even)
    def _():
        pl.semaphore_wait(entered_sem, columns)

    for f in range(2, 4):
        pl.when(jnp.logical_and(even, present[f]))(faces[f].start)

    own = double_layer(256)
    send_sums.wait_recv()
    for half in range(2):
        bem_ref[half : half + 1, :] = (
            own[half] + sums_in[half : half + 1, :]
        ) * (1.0 / FOUR_PI) - 0.5 * target_trace[half : half + 1, :]

    send_spots.wait_send()
    send_sums.wait_send()

    for f in range(4):
        pl.when(present[f])(faces[f].wait_send)
    for f in range(4):
        pl.when(present[f])(faces[f ^ 1].wait_recv)

        @pl.when(jnp.logical_not(present[f]))
        def _():
            incoming[f] = jnp.zeros((2, 128), F32)

    index_rows, value_rows = [], []
    for f in range(4):
        for half in range(2):
            row = 4 * half + f
            index_rows.append(face_ref[row : row + 1, :])
            value_rows.append(incoming[f, half : half + 1, :])
    fem_ref[...] = partial[...] + as_table(scatter_product(index_rows, value_rows))


def per_device(
    nodal_field, element_matrix, connectivity, face_nodes, panel_node, panel_weight,
    centroid, panel_normal, panel_count, target_index, round_owner,
):
    vmem = pl.BlockSpec(memory_space=pltpu.VMEM)
    hbm = pl.BlockSpec(memory_space=pl.ANY)
    i32 = jnp.int32
    connect = connectivity[0, 0].reshape(4, 128, 128).transpose(1, 0, 2).reshape(ROWS, 128)
    faces = face_nodes[0, 0].reshape(4, 2, 128).transpose(1, 0, 2).reshape(8, 128)
    fem, bem = pl.pallas_call(
        kernel,
        out_shape=(
            pltpu.VMEM((HI, LO), F32),
            pltpu.VMEM((2, 128), F32),
        ),
        in_specs=[hbm] * 11,
        out_specs=(vmem, vmem),
        scratch_shapes=[
            pltpu.SMEM((GY, GX), i32),
            pltpu.SMEM((ROUNDS,), i32),
            pltpu.VMEM((HI, LO), F32),
            pltpu.VMEM((ROWS, 128), i32),
            pltpu.VMEM((16, ROWS * 32), F32),
            pltpu.VMEM((8, 128), i32),
            pltpu.VMEM((4, 128), i32),
            pltpu.VMEM((4, 128), F32),
            pltpu.VMEM((3, 4, 128), F32),
            pltpu.VMEM((3, 4, 128), F32),
            pltpu.VMEM((2, 128), i32),
            pltpu.VMEM((2, 12, 128), F32),
            pltpu.VMEM((GX, 12, 128), F32),
            pltpu.VMEM((8 * PAIRS, 128), F32),
            pltpu.VMEM((2 * BINS, BINS), F32),
            pltpu.VMEM((HI, LO), F32),
            pltpu.VMEM((4, 2, 128), F32),
            pltpu.VMEM((4, 2, 128), F32),
            pltpu.VMEM((6, 128), F32),
            pltpu.VMEM((6, 128), F32),
            pltpu.VMEM((3, 512, 128), F32),
            pltpu.VMEM((256, 128), F32),
            pltpu.VMEM((2, 128), F32),
            pltpu.VMEM((2, 128), F32),
            pltpu.SemaphoreType.DMA((9,)),
            pltpu.SemaphoreType.DMA((STEPS,)),
            pltpu.SemaphoreType.DMA((STEPS,)),
            pltpu.SemaphoreType.DMA((GX,)),
            pltpu.SemaphoreType.DMA((GX,)),
            pltpu.SemaphoreType.DMA((4,)),
            pltpu.SemaphoreType.DMA((4,)),
            pltpu.SemaphoreType.DMA((2,)),
            pltpu.SemaphoreType.DMA((2,)),
            pltpu.SemaphoreType.REGULAR,
        ],
        compiler_params=pltpu.CompilerParams(
            collective_id=0, has_side_effects=True, vmem_limit_bytes=60 * 1024 * 1024
        ),
        name="apply",
    )(
        panel_count.T,
        round_owner,
        nodal_field.reshape(HI, LO),
        connect,
        element_matrix.reshape(16, -1),
        faces,
        panel_node.reshape(4, 128),
        panel_weight.reshape(4, 128),
        centroid.transpose(0, 2, 1, 3).reshape(3, 4, 128),
        panel_normal.transpose(0, 2, 1, 3).reshape(3, 4, 128),
        target_index.reshape(2, 128),
    )
    return fem.reshape(1, 1, HI * LO), bem.reshape(1, 1, 256)


def solution(mesh):
    split = P("px", "py")
    return jax.shard_map(
        per_device,
        mesh=mesh,
        in_specs=(split,) * 8 + (P(), split, P()),
        out_specs=(split, split),
        check_vma=False,
    )
```

```python
import functools
import math

import jax
import jax.numpy as jnp
from jax import lax
from jax.experimental import pallas as pl
from jax.experimental.pallas import tpu as pltpu
from jax.sharding import PartitionSpec as P

F32 = jnp.float32
BF16 = jnp.bfloat16
MESH = pl.DeviceIdType.MESH

GX, GY = 32, 8
ROUNDS = 8
BINS = 64
ROWS = 512
HI, LO = 32, 128
PAIRS = 32
STEPS = ROWS // (8 * PAIRS)
GROUPS = 8
SMOOTH_SQ = 0.01
FOUR_PI = 4.0 * math.pi


def lookup(rows, index):
    lo, hi = index & (LO - 1), index >> 7
    total = jnp.zeros(index.shape, F32)
    for r, row in enumerate(rows):
        picked = jnp.take_along_axis(jnp.broadcast_to(row, index.shape), lo, axis=1)
        total = jnp.where(hi == r, picked, total)
    return total


def table(ref):
    return [ref[r : r + 1, :] for r in range(HI)]


def stack(x, count):
    return jnp.concatenate([x] * count, axis=0)


def one_hots(index_rows, value_rows):
    bins = lax.broadcasted_iota(jnp.int32, (BINS, 128), 0).astype(F32).astype(BF16)
    zero, one = jnp.zeros((BINS, 128), BF16), jnp.ones((BINS, 128), BF16)
    left, right = [], []
    for index, value in zip(index_rows, value_rows):
        hi = (index >> 7) | ((index & 64) >> 1)
        hi = jnp.broadcast_to(hi.astype(F32), (16, 128)).astype(BF16)
        lo = jnp.broadcast_to((index & 63).astype(F32), (16, 128)).astype(BF16)
        value = jnp.broadcast_to(value, (16, 128))
        upper = value.astype(BF16)
        lower = (value - upper.astype(F32)).astype(BF16)
        at_hi = stack(hi, BINS // 16) == bins
        left.append(
            jnp.concatenate(
                [
                    jnp.where(at_hi, stack(upper, BINS // 16), zero),
                    jnp.where(at_hi, stack(lower, BINS // 16), zero),
                ],
                axis=0,
            )
        )
        right.append(jnp.where(stack(lo, BINS // 16) == bins, one, zero))
    return jnp.concatenate(left, axis=1), jnp.concatenate(right, axis=1)


def scatter_product(index_rows, value_rows):
    left, right = one_hots(index_rows, value_rows)
    return lax.dot_general(left, right, (((1,), (1,)), ((), ())), preferred_element_type=F32)


def as_table(sums):
    bins = sums[0:BINS, :] + sums[BINS : 2 * BINS, :]
    return jnp.concatenate([bins[0:HI, :], bins[HI:BINS, :]], axis=1)


def kernel(
    count_hbm, owner_hbm, nodal_hbm, conn_hbm, matrix_hbm, face_hbm, node_hbm, weight_hbm,
    centroid_hbm, normal_hbm, target_hbm,
    fem_ref, bem_ref,
    count_ref, owner_ref, nodal_ref, conn_ref, matrix_ref, face_ref, node_ref, weight_ref,
    centroid_ref, normal_ref, target_ref,
    halves, gathered, value, total, partial, sent, incoming, spots_out, spots_in, place,
    potential, sums_out, sums_in,
    load_sem, conn_sem, matrix_sem, send_sem, recv_sem, face_send, face_recv, pair_send, pair_recv, entered_sem,
):
    px, py = lax.axis_index("px"), lax.axis_index("py")
    core = px & 1
    sibling = px + 1 - 2 * core
    low_y, high_y = (py + GY - 1) & (GY - 1), (py + 1) & (GY - 1)

    names = ("nodal", "node", "count", "weight", "centroid", "normal", "target", "face", "owner")
    sources = (nodal_hbm, node_hbm, count_hbm, weight_hbm, centroid_hbm, normal_hbm, target_hbm, face_hbm, owner_hbm)
    places = (nodal_ref, node_ref, count_ref, weight_ref, centroid_ref, normal_ref, target_ref, face_ref, owner_ref)
    loads = {
        name: pltpu.make_async_copy(source, where, load_sem.at[i])
        for i, (name, source, where) in enumerate(zip(names, sources, places))
    }

    def conn_load(step):
        rows = pl.ds(pl.multiple_of(step * 8 * PAIRS, 8), 8 * PAIRS)
        return pltpu.make_async_copy(conn_hbm.at[rows], conn_ref.at[rows], conn_sem.at[step])

    def matrix_load(step):
        lanes = pl.ds(pl.multiple_of(step * 256 * PAIRS, 128), 256 * PAIRS)
        return pltpu.make_async_copy(
            matrix_hbm.at[:, lanes], matrix_ref.at[:, lanes], matrix_sem.at[step]
        )

    for name in names:
        loads[name].start()

    @pl.loop(0, STEPS)
    def _(step):
        conn_load(step).start()
        matrix_load(step).start()

    barrier = pltpu.get_barrier_semaphore()

    @pl.loop(1, GX)
    def _(d):
        pl.semaphore_signal(
            barrier, inc=1, device_id=((px + d) & (GX - 1), py), device_id_type=MESH
        )

    even = (py & 1) == 0
    late = jnp.logical_not(even)
    present = (px > 0, px < GX - 1, py > 0, py < GY - 1)
    columns = present[2].astype(jnp.int32) + present[3].astype(jnp.int32)

    def greet(semaphore, ours):
        for column, there in ((low_y, present[2]), (high_y, present[3])):

            @pl.when(jnp.logical_and(ours, there))
            def _():
                pl.semaphore_signal(
                    semaphore, inc=1, device_id=(px, column), device_id_type=MESH
                )

    greet(barrier, even)

    sublane = lax.broadcasted_iota(jnp.int32, (8, 128), 0)
    lane = lax.broadcasted_iota(jnp.int32, (8, 128), 1)

    loads["nodal"].wait()
    for name in ("node", "count", "weight", "centroid", "normal", "target"):
        loads[name].wait()
    trace = lookup(table(nodal_ref), stack(node_ref[...], 2))
    live = count_ref[py, px]
    slot = (sublane & 3) * 128 + lane
    weighted = jnp.where(slot < live, stack(weight_ref[...], 2) * trace, 0.0)
    for h in range(2):
        for c in range(3):
            halves[h, 2 * c : 2 * c + 2, :] = centroid_ref[c, 2 * h : 2 * h + 2, :]
            halves[h, 6 + 2 * c : 8 + 2 * c, :] = (
                normal_ref[c, 2 * h : 2 * h + 2, :] * weighted[2 * h : 2 * h + 2, :]
            )

    targets = stack(target_ref[...], 4)
    target_trace = lookup([trace[k : k + 1, :] for k in range(2)], targets)
    for c in range(3):
        where = lookup([centroid_ref[c, k : k + 1, :] for k in range(2)], targets)
        spots_out[2 * c : 2 * c + 2, :] = where[0:2, :]

    total[...] = jnp.zeros_like(total)
    odd, second, fourth = (sublane & 1) == 1, (sublane & 2) == 2, (sublane & 4) == 4

    def elements(step):
        conn_load(step).wait()
        matrix_load(step).wait()
        base = step * PAIRS
        index_rows, value_rows = [], []
        for u in range(PAIRS):
            at = pl.multiple_of((base + u) * 8, 8)
            nodes = conn_ref[pl.ds(at, 8), :]
            values = lookup(table(nodal_ref), nodes)
            swapped = pltpu.roll(values, 4, 0)
            folded = []
            for chunk in range(2):
                pair = (swapped, values) if chunk == 0 else (values, swapped)
                both = jnp.where(fourth, *pair)
                lanes = pl.ds(pl.multiple_of((base + u) * 256 + 128 * chunk, 128), 128)
                first = matrix_ref[0:8, lanes] * both
                last = matrix_ref[8:16, lanes] * both
                folded.append(
                    jnp.where(second, last + pltpu.roll(last, 2, 0), first + pltpu.roll(first, 6, 0))
                )
            value[8 * u : 8 * u + 8, :] = jnp.where(
                odd, folded[1] + pltpu.roll(folded[1], 1, 0), folded[0] + pltpu.roll(folded[0], 7, 0)
            )
            for chunk in range(2):
                for corner in range(4):
                    index_rows.append(conn_ref[pl.ds(at + 4 * chunk + corner, 1), :])
                    row = 8 * u + (0, 4, 2, 6)[corner] + chunk
                    value_rows.append(value[row : row + 1, :])
        total[...] += scatter_product(index_rows, value_rows)

    ahead = 1
    pl.loop(0, ahead)(elements)

    pl.semaphore_wait(barrier, GX - 1 + columns * (py & 1))
    greet(entered_sem, late)

    def to_other(d, source):
        target = (px + d) & (GX - 1)
        return pltpu.make_async_remote_copy(
            src_ref=halves.at[target & 1],
            dst_ref=gathered.at[source],
            send_sem=send_sem.at[d],
            recv_sem=recv_sem.at[source],
            device_id=(target, py),
            device_id_type=MESH,
        )

    def to_sibling(source, where, n):
        return pltpu.make_async_remote_copy(
            src_ref=source,
            dst_ref=where,
            send_sem=pair_send.at[n],
            recv_sem=pair_recv.at[n],
            device_id=(sibling, py),
            device_id_type=MESH,
        )

    send_spots = to_sibling(spots_out, spots_in, 0)
    send_sums = to_sibling(sums_out, sums_in, 1)

    @pl.loop(1, GX)
    def _(d):
        to_other(d, px).start()

    send_spots.start()
    gathered[px] = halves[core]

    def spread(ref, first):
        for c in range(3):
            for half in range(2):
                row = ref[2 * c + half : 2 * c + half + 1, :]
                rows = slice(first + 128 * half, first + 128 * half + 128)
                place[c, rows, :] = jnp.broadcast_to(row, (128, 128)).T

    pl.loop(ahead, STEPS)(elements)

    partial[...] = as_table(total[...])

    loads["face"].wait()
    outgoing = lookup(table(partial), face_ref[...])
    for f in range(4):
        for half in range(2):
            sent[f, half : half + 1, :] = outgoing[4 * half + f : 4 * half + f + 1, :]
    neighbours = (
        ((px + GX - 1) & (GX - 1), py),
        ((px + 1) & (GX - 1), py),
        (px, low_y),
        (px, high_y),
    )
    faces = [
        pltpu.make_async_remote_copy(
            src_ref=sent.at[f],
            dst_ref=incoming.at[f ^ 1],
            send_sem=face_send.at[f],
            recv_sem=face_recv.at[f ^ 1],
            device_id=neighbours[f],
            device_id_type=MESH,
        )
        for f in range(4)
    ]
    for f in range(2):
        pl.when(present[f])(faces[f].start)
    for f in range(2, 4):
        pl.when(jnp.logical_and(late, present[f]))(faces[f].start)

    loads["owner"].wait()
    spread(spots_out, 256)
    send_spots.wait_recv()
    spread(spots_in, 0)

    @pl.loop(1, GX)
    def _(d):
        to_other(d, px).wait_send()

    @pl.loop(1, GX)
    def _(d):
        to_other(d, (px + GX - d) & (GX - 1)).wait_recv()

    def double_layer(first):
        @pl.loop(0, 32 // GROUPS)
        def _(part):
            at = [pl.multiple_of(8 * (GROUPS * part + g), 8) for g in range(GROUPS)]
            spots = [[place[c, pl.ds(first + at[g], 8), :] for c in range(3)] for g in range(GROUPS)]

            def one_round(r, sums):
                owner = owner_ref[r]
                sums = list(sums)
                for k in range(2):
                    rows = [
                        jnp.broadcast_to(gathered[owner, 2 * c + k : 2 * c + k + 1, :], (8, 128))
                        for c in range(6)
                    ]
                    for g in range(GROUPS):
                        dx, dy, dz = (spots[g][c] - rows[c] for c in range(3))
                        inverse = lax.rsqrt(dx * dx + dy * dy + dz * dz + SMOOTH_SQ)
                        along = rows[3] * dx + rows[4] * dy + rows[5] * dz
                        sums[g] = sums[g] + along * (inverse * inverse * inverse)
                return tuple(sums)

            sums = lax.fori_loop(
                0, ROUNDS, one_round, (jnp.zeros((8, 128), F32),) * GROUPS, unroll=2
            )
            for g in range(GROUPS):
                potential[pl.ds(at[g], 8), :] = sums[g]

        return [
            jnp.sum(potential[128 * half : 128 * half + 128, :].T, axis=0, keepdims=True)
            for half in range(2)
        ]

    for half, row in enumerate(double_layer(0)):
        sums_out[half : half + 1, :] = row
    send_sums.start()

    @pl.when(even)
    def _():
        pl.semaphore_wait(entered_sem, columns)

    for f in range(2, 4):
        pl.when(jnp.logical_and(even, present[f]))(faces[f].start)

    own = double_layer(256)
    send_sums.wait_recv()
    for half in range(2):
        bem_ref[half : half + 1, :] = (
            own[half] + sums_in[half : half + 1, :]
        ) * (1.0 / FOUR_PI) - 0.5 * target_trace[half : half + 1, :]

    send_spots.wait_send()
    send_sums.wait_send()

    for f in range(4):
        pl.when(present[f])(faces[f].wait_send)
    for f in range(4):
        pl.when(present[f])(faces[f ^ 1].wait_recv)

        @pl.when(jnp.logical_not(present[f]))
        def _():
            incoming[f] = jnp.zeros((2, 128), F32)

    index_rows, value_rows = [], []
    for f in range(4):
        for half in range(2):
            row = 4 * half + f
            index_rows.append(face_ref[row : row + 1, :])
            value_rows.append(incoming[f, half : half + 1, :])
    fem_ref[...] = partial[...] + as_table(scatter_product(index_rows, value_rows))


def per_device(
    nodal_field, element_matrix, connectivity, face_nodes, panel_node, panel_weight,
    centroid, panel_normal, panel_count, target_index, round_owner,
):
    vmem = pl.BlockSpec(memory_space=pltpu.VMEM)
    hbm = pl.BlockSpec(memory_space=pl.ANY)
    i32 = jnp.int32
    connect = connectivity[0, 0].reshape(4, 128, 128).transpose(1, 0, 2).reshape(ROWS, 128)
    faces = face_nodes[0, 0].reshape(4, 2, 128).transpose(1, 0, 2).reshape(8, 128)
    fem, bem = pl.pallas_call(
        kernel,
        out_shape=(
            pltpu.VMEM((HI, LO), F32),
            pltpu.VMEM((2, 128), F32),
        ),
        in_specs=[hbm] * 11,
        out_specs=(vmem, vmem),
        scratch_shapes=[
            pltpu.SMEM((GY, GX), i32),
            pltpu.SMEM((ROUNDS,), i32),
            pltpu.VMEM((HI, LO), F32),
            pltpu.VMEM((ROWS, 128), i32),
            pltpu.VMEM((16, ROWS * 32), F32),
            pltpu.VMEM((8, 128), i32),
            pltpu.VMEM((4, 128), i32),
            pltpu.VMEM((4, 128), F32),
            pltpu.VMEM((3, 4, 128), F32),
            pltpu.VMEM((3, 4, 128), F32),
            pltpu.VMEM((2, 128), i32),
            pltpu.VMEM((2, 12, 128), F32),
            pltpu.VMEM((GX, 12, 128), F32),
            pltpu.VMEM((8 * PAIRS, 128), F32),
            pltpu.VMEM((2 * BINS, BINS), F32),
            pltpu.VMEM((HI, LO), F32),
            pltpu.VMEM((4, 2, 128), F32),
            pltpu.VMEM((4, 2, 128), F32),
            pltpu.VMEM((6, 128), F32),
            pltpu.VMEM((6, 128), F32),
            pltpu.VMEM((3, 512, 128), F32),
            pltpu.VMEM((256, 128), F32),
            pltpu.VMEM((2, 128), F32),
            pltpu.VMEM((2, 128), F32),
            pltpu.SemaphoreType.DMA((9,)),
            pltpu.SemaphoreType.DMA((STEPS,)),
            pltpu.SemaphoreType.DMA((STEPS,)),
            pltpu.SemaphoreType.DMA((GX,)),
            pltpu.SemaphoreType.DMA((GX,)),
            pltpu.SemaphoreType.DMA((4,)),
            pltpu.SemaphoreType.DMA((4,)),
            pltpu.SemaphoreType.DMA((2,)),
            pltpu.SemaphoreType.DMA((2,)),
            pltpu.SemaphoreType.REGULAR,
        ],
        compiler_params=pltpu.CompilerParams(
            collective_id=0, has_side_effects=True, vmem_limit_bytes=60 * 1024 * 1024
        ),
        name="apply",
    )(
        panel_count.T,
        round_owner,
        nodal_field.reshape(HI, LO),
        connect,
        element_matrix.reshape(16, -1),
        faces,
        panel_node.reshape(4, 128),
        panel_weight.reshape(4, 128),
        centroid.transpose(0, 2, 1, 3).reshape(3, 4, 128),
        panel_normal.transpose(0, 2, 1, 3).reshape(3, 4, 128),
        target_index.reshape(2, 128),
    )
    return fem.reshape(1, 1, HI * LO), bem.reshape(1, 1, 256)


def solution(mesh):
    split = P("px", "py")
    return jax.shard_map(
        per_device,
        mesh=mesh,
        in_specs=(split,) * 8 + (P(), split, P()),
        out_specs=(split, split),
        check_vma=False,
    )
```
